128 devices in a mesh: dp: 16 (over y_lo, z, core), tensor: 8 (over x, y_hi).
Axes of the slice: x: 4, y: 4 (y_hi: 2, y_lo: 2; y = y_hi * 2 + y_lo), z: 4, core: 2. Of those that a mesh axis runs over, the one named last changes fastest.
Arguments:
- normed: bfloat16 [8192, 8192], P('dp', 'tensor'), may hold values from -6 to 6
- query_back: bfloat16 [8192, 4096], P('dp', 'tensor'), may hold values from -1.5 to 1.5
- key_back: bfloat16 [8192, 1024], P('dp', 'tensor'), may hold values from -3 to 3
- value_back: bfloat16 [8192, 1024], P('dp', 'tensor'), may hold values from -3 to 3
- query_proj: bfloat16 [8192, 4096], P(None, 'tensor'), may hold values from -0.0625 to 0.0625
- key_proj: bfloat16 [8192, 1024], P(None, 'tensor'), may hold values from -0.0625 to 0.0625
- value_proj: bfloat16 [8192, 1024], P(None, 'tensor'), may hold values from -0.0625 to 0.0625
- source: int32 [4096], replicated, may hold values from 0 to 8191, as said below
Outputs:
- query_grad: float32 [8192, 4096], P('dp', 'tensor')
- key_grad: float32 [8192, 1024], P('dp', 'tensor')
- value_grad: float32 [8192, 1024], P('dp', 'tensor')
- input_grad: float32 [4096, 8192], P('dp', 'tensor')
The draws below stay inside these ranges and needn't reach their ends.
Inputs may be any that keep to these rules, and one draw needn't show every extreme that they name: Each arrival device of the dp axis holds its live rows in its first slots; every live slot appears exactly once in source, no other slot appears. Every balanced device takes the same number of rows from a given arrival device, in one run of consecutive slots, runs ordered by arrival device; this number is at most 32 and equals 32 for at least one arrival device. Each balanced device holds 256 rows.
All inputs are finite; a program needn't handle non-finite values.
Results may differ from the reference program's by a relative error of at most 0.0003.
Values may be sent and summed in bfloat16 or wider, within the bound.
No kernel may reach another device: no remote copies, remote signals or barrier semaphores. Data moves between devices by JAX's collectives and lax.ppermute only.
A program may use at most 192 MiB of HBM per device.

```python
import jax
import jax.numpy as jnp
from jax import lax

D = 8192
CAP = 512
QW = 4096
KVW = 1024
BAL = 256
TOK_ARR = 8192
TOKENS = 4096
N_DP = 16
N_TENSOR = 8


def draw_source(key, part):
    key = jax.random.fold_in(key, 11)
    unit_most = CAP // N_DP
    others = N_DP - 1
    key_full, key_units, key_order = jax.random.split(key, 3)
    full_index = jax.random.randint(key_full, (), 0, N_DP).astype(jnp.int32)
    shuffled = jax.random.permutation(key_units, others * unit_most).astype(jnp.int32)
    chosen = shuffled[:BAL - unit_most]
    others_ids = jnp.arange(others, dtype=jnp.int32)
    taken = jnp.sum((chosen[:, None] // unit_most == others_ids[None, :]).astype(jnp.int32), axis=0)
    device_ids = jnp.arange(N_DP, dtype=jnp.int32)
    position = jnp.where(device_ids < full_index, device_ids, device_ids - 1)
    spread_units = jnp.sum(jnp.where(position[:, None] == others_ids[None, :], taken[None, :], 0), axis=1)
    units = jnp.where(device_ids == full_index, unit_most, spread_units).astype(jnp.int32)
    live_rows = units * N_DP
    row_ids = jnp.arange(CAP, dtype=jnp.int32)
    scores = jax.random.randint(key_order, (N_DP, CAP), 0, 2 ** 20).astype(jnp.int32)
    keyed = jnp.where(row_ids[None, :] < live_rows[:, None], scores, 2 ** 21 + row_ids[None, :])
    order_rows = jnp.argsort(keyed, axis=1, stable=True).astype(jnp.int32)
    run_ends = jnp.cumsum(units).astype(jnp.int32)
    run_starts = run_ends - units
    slot_ids = jnp.arange(BAL, dtype=jnp.int32)
    owners = jnp.sum((run_ends[None, :] <= slot_ids[:, None]).astype(jnp.int32), axis=1)
    within = slot_ids - run_starts[owners]
    picks = within[None, :] * N_DP + device_ids[:, None]
    owner_order = order_rows[owners]
    chosen_rows = jnp.take_along_axis(owner_order, picks.T, axis=1).T
    entries = owners[None, :] * CAP + chosen_rows
    return entries.reshape(-1).astype(jnp.int32)


def strengthened(values, rng, source, target, blocks, factor):
    owner, partner = [(jnp.arange(values.shape[dim]) // (values.shape[dim] // blocks)).reshape([-1 if axis == dim else 1 for axis in range(values.ndim)]) for dim in (source, target)]
    chosen = jax.random.permutation(rng, blocks)[partner]
    strong = (owner == chosen) | (owner == (partner + blocks // 2) % blocks)
    return jnp.where(strong, factor * values, values)


def block_scale(rng, shape, pieces, smallest, top_value):
    gain, own = 1.0, jax.random.fold_in(rng, 6)
    for axis_at, blocks in pieces:
        steps = jnp.exp(jax.random.uniform(jax.random.fold_in(own, axis_at), (blocks,), jnp.float32, smallest / len(pieces), top_value / len(pieces)))
        gain = gain * jnp.repeat(steps, shape[axis_at] // blocks).reshape([-1 if axis == axis_at else 1 for axis in range(len(shape))])
    return gain


def scatter_about(key, shape, width, most, pieces=(), held_as=jnp.bfloat16):
    result = width * jax.random.normal(key, shape, jnp.float32)
    if pieces:
        result = result * block_scale(key, shape, pieces, -0.22, 0.18)
    return jnp.clip(result, -most, most).astype(held_as)


def gaussian_with(own_key, dims, spread, most, pieces, heavy, kind=jnp.bfloat16):
    array = spread * jax.random.normal(own_key, dims, jnp.float32)
    if pieces:
        array = array * block_scale(own_key, dims, pieces, -0.22, 0.18)
    return jnp.clip(strengthened(array, jax.random.fold_in(own_key, 3), *heavy), -most, most).astype(kind)


def setup_inputs(seed: int = 0) -> dict:
    seeds = jax.random.split(jax.random.key(seed), 9)
    return {
        "normed": gaussian_with(seeds[0], (TOK_ARR, D), 1.0, 6.0, ((0, 16), (1, 8)), (0, 1, 16, 2.0)),
        "query_back": scatter_about(seeds[1], (TOK_ARR, QW), 0.25, 1.5, ((0, 16), (1, 8))),
        "key_back": scatter_about(seeds[2], (TOK_ARR, KVW), 0.5, 3.0, ((0, 16), (1, 8))),
        "value_back": scatter_about(seeds[3], (TOK_ARR, KVW), 0.5, 3.0, ((0, 16), (1, 8))),
        "query_proj": scatter_about(seeds[4], (D, QW), D ** -0.5, 0.0625, ((1, 8),)),
        "key_proj": scatter_about(seeds[5], (D, KVW), D ** -0.5, 0.0625, ((1, 8),)),
        "value_proj": scatter_about(seeds[6], (D, KVW), D ** -0.5, 0.0625, ((1, 8),)),
        "source": draw_source(jax.random.fold_in(seeds[8], 71), 0),
    }


def reference(normed, query_back, key_back, value_back, query_proj, key_proj, value_proj, source):
    inputs_taken = normed[source]
    query_taken = query_back[source]
    key_taken = key_back[source]
    value_taken = value_back[source]
    back_rows = jnp.concatenate([query_taken, key_taken, value_taken], axis=1)
    weight_grad = jnp.dot(inputs_taken.T, back_rows, preferred_element_type=jnp.float32)
    query_group = QW // N_TENSOR
    key_group = KVW // N_TENSOR
    contract = (((1,), (1,)), ((), ()))

    def add_group(summed, group_index):
        first_query = group_index * query_group
        first_key = group_index * key_group
        part_sum = lax.dot_general(lax.dynamic_slice_in_dim(query_taken, first_query, query_group, 1),
                                   lax.dynamic_slice_in_dim(query_proj, first_query, query_group, 1),
                                   contract, preferred_element_type=jnp.float32)
        part_sum = part_sum + lax.dot_general(lax.dynamic_slice_in_dim(key_taken, first_key, key_group, 1),
                                              lax.dynamic_slice_in_dim(key_proj, first_key, key_group, 1),
                                              contract, preferred_element_type=jnp.float32)
        part_sum = part_sum + lax.dot_general(lax.dynamic_slice_in_dim(value_taken, first_key, key_group, 1),
                                              lax.dynamic_slice_in_dim(value_proj, first_key, key_group, 1),
                                              contract, preferred_element_type=jnp.float32)
        return summed + part_sum, None

    summed, _ = lax.scan(add_group, jnp.zeros((TOKENS, D), jnp.float32), jnp.arange(N_TENSOR, dtype=jnp.int32))
    return (weight_grad[:, :QW], weight_grad[:, QW:QW + KVW], weight_grad[:, QW + KVW:], summed)
```

```python
import jax
import jax.numpy as jnp
from jax import lax
from jax.experimental import pallas as pl
from jax.experimental.pallas import tpu as pltpu
from jax.sharding import Mesh, PartitionSpec as P

CORES = 2
SCALE_ROWS = 16
FRACTION_BITS = 15


def relay_plan(source, capacity, dp_count, my_index):
    balanced = source.shape[0] // dp_count
    per_pair = capacity // dp_count
    slot_table = source.reshape(dp_count, balanced)
    owners = slot_table[0] // capacity
    devices = jnp.arange(dp_count, dtype=jnp.int32)
    member = owners[:, None] == devices[None, :]
    counts = jnp.sum(member.astype(jnp.int32), axis=0)
    starts = jnp.cumsum(counts) - counts
    is_mine = devices == my_index
    my_start = jnp.sum(jnp.where(is_mine, starts, 0))
    my_count = jnp.sum(jnp.where(is_mine, counts, 0))
    padded = jnp.concatenate([slot_table, jnp.zeros((dp_count, per_pair), jnp.int32)], axis=1)
    picked = lax.dynamic_slice_in_dim(padded, my_start, per_pair, 1) - my_index * capacity
    valid = jnp.arange(per_pair, dtype=jnp.int32)[None, :] < my_count
    local_rows = jnp.where(valid, picked, -1).reshape(-1)
    slot_index = jnp.arange(balanced, dtype=jnp.int32)
    owner_start = jnp.sum(jnp.where(member, starts[None, :], 0), axis=1)
    flat_slots = owners * per_pair + slot_index - owner_start
    return local_rows, flat_slots


def take_rows(values, rows):
    chosen = (rows[:, None] == jnp.arange(values.shape[0], dtype=jnp.int32)[None, :]).astype(values.dtype)
    return jnp.dot(chosen, values, preferred_element_type=jnp.float32).astype(values.dtype)


def partial_kernel(rows_ref, query_ref, key_ref, value_ref, out_ref):
    contract = (((1,), (1,)), ((), ()))
    query_width = query_ref.shape[1]
    tokens = rows_ref.shape[0]
    part = lax.dot_general(
        rows_ref[:, :query_width], query_ref[...], contract, preferred_element_type=jnp.float32
    )
    others = jnp.concatenate([key_ref[...], value_ref[...]], axis=1)
    part = part + lax.dot_general(
        rows_ref[:, query_width:], others, contract, preferred_element_type=jnp.float32
    )
    most = jnp.max(jnp.abs(part), axis=1, keepdims=True)
    exponent = jnp.floor(jnp.log2(jnp.maximum(most, 2.0**-100))) + 1.0
    coded = jnp.round(part * jnp.exp2(FRACTION_BITS - exponent))
    coded = jnp.clip(coded, -32767.0, 32767.0)
    out_ref[0, :tokens, :] = coded.astype(jnp.int32).astype(jnp.int16)
    across = jnp.transpose(jnp.broadcast_to(exponent, (tokens, 128)))[:SCALE_ROWS, :]
    width = out_ref.shape[2]
    across = jnp.concatenate([across, jnp.zeros((SCALE_ROWS, width - tokens), jnp.float32)], axis=1)
    out_ref[0, tokens:, :] = across.astype(jnp.int32).astype(jnp.int16)


def coded_partials(rows, query_proj, key_proj, value_proj, blocks):
    tokens, width = rows.shape
    features = query_proj.shape[0] // blocks
    query_width, key_width = query_proj.shape[1], key_proj.shape[1]
    return pl.pallas_call(
        partial_kernel,
        grid=(blocks,),
        in_specs=[
            pl.BlockSpec((tokens, width), lambda g: (0, 0)),
            pl.BlockSpec((features, query_width), lambda g: (g, 0)),
            pl.BlockSpec((features, key_width), lambda g: (g, 0)),
            pl.BlockSpec((features, key_width), lambda g: (g, 0)),
        ],
        out_specs=pl.BlockSpec((1, tokens + SCALE_ROWS, features), lambda g: (g, 0, 0)),
        out_shape=jax.ShapeDtypeStruct((blocks, tokens + SCALE_ROWS, features), jnp.int16),
        compiler_params=pltpu.CompilerParams(vmem_limit_bytes=40 * 2**20),
    )(rows, query_proj, key_proj, value_proj)


def decoded_sum(arrived, tokens):
    exponent = arrived[:, tokens, :tokens].astype(jnp.float32)
    step = jnp.exp2(exponent - FRACTION_BITS)[:, :, None]
    return jnp.sum(arrived[:, :tokens, :].astype(jnp.float32) * step, axis=0)


def body(normed, query_back, key_back, value_back, query_proj, key_proj, value_proj, source):
    chips = lax.axis_size("chip")
    groups = lax.axis_size("tensor")
    dp_count = chips * CORES
    core = lax.axis_index("core")
    my_index = lax.axis_index("chip") * CORES + core
    capacity, features = normed.shape
    per_pair = capacity // dp_count
    tokens = source.shape[0] // dp_count
    query_width, key_width = query_back.shape[1], key_back.shape[1]
    local_rows, flat_slots = relay_plan(source, capacity, dp_count, my_index)

    packed = take_rows(normed, local_rows).reshape(groups, -1, features)
    spread = lax.all_to_all(packed, "tensor", split_axis=0, concat_axis=0, tiled=True)
    spread = spread.reshape(dp_count, per_pair, features)
    back_rows = jnp.concatenate([query_back, key_back, value_back], axis=1)
    back_packed = take_rows(back_rows, local_rows).reshape(dp_count, per_pair, -1)
    relayed = lax.all_to_all(
        jnp.concatenate([spread, back_packed], axis=2), ("chip", "core"), split_axis=0, concat_axis=0, tiled=True
    )
    balanced = take_rows(relayed.reshape(dp_count * per_pair, -1), flat_slots)
    inputs_mine, back_mine = balanced[:, :features], balanced[:, features:]

    inputs_all = lax.all_gather(inputs_mine, "tensor", axis=0, tiled=True)
    coded = coded_partials(back_mine, query_proj, key_proj, value_proj, groups)
    arrived = lax.all_to_all(coded, "tensor", split_axis=0, concat_axis=0, tiled=True)
    input_grad = decoded_sum(arrived, tokens)

    copies = jnp.broadcast_to(back_mine[None], (chips,) + back_mine.shape)
    back_all = lax.all_to_all(copies, "chip", split_axis=0, concat_axis=0, tiled=True)
    back_all = back_all.reshape(chips * tokens, -1)

    half = features // CORES

    def half_grad(which):
        part = lax.dynamic_slice_in_dim(inputs_all, which * half, half, 1)
        return lax.dot_general(part, back_all, (((0,), (0,)), ((), ())), preferred_element_type=jnp.float32)

    other = lax.ppermute(half_grad(1 - core), "core", [(0, 1), (1, 0)])
    weight_grad = half_grad(core) + other
    return (
        weight_grad[:, :query_width],
        weight_grad[:, query_width : query_width + key_width],
        weight_grad[:, query_width + key_width :],
        input_grad,
    )


def solution(mesh):
    dp_count, groups = mesh.shape["dp"], mesh.shape["tensor"]
    by_chip = Mesh(mesh.devices.reshape(dp_count // CORES, CORES, groups), ("chip", "core", "tensor"))
    dp = ("chip", "core")
    in_specs = (
        P(dp, "tensor"),
        P(dp, "tensor"),
        P(dp, "tensor"),
        P(dp, "tensor"),
        P(None, "tensor"),
        P(None, "tensor"),
        P(None, "tensor"),
        P(),
    )
    out_specs = (P(dp, "tensor"), P(dp, "tensor"), P(dp, "tensor"), P(dp, "tensor"))
    return jax.shard_map(body, mesh=by_chip, in_specs=in_specs, out_specs=out_specs, check_vma=False)
```

```python
import functools
import itertools

import jax
import jax.numpy as jnp
from jax import lax
from jax.experimental import pallas as pl
from jax.experimental.pallas import tpu as pltpu
from jax.sharding import Mesh, PartitionSpec as P

DP_SIZES = (("y_lo", 2), ("z", 4), ("core", 2))
TENSOR_SIZES = (("x", 4), ("y_hi", 2))
DP = tuple(name for name, _ in DP_SIZES)
TENSOR = tuple(name for name, _ in TENSOR_SIZES)
SCALE_ROWS = 16
FRACTION_BITS = 15


def balanced_slots(source, dp_count, per_pair):
    owners = source[: source.shape[0] // dp_count] // (dp_count * per_pair)
    owner_start = jnp.sum((owners[None, :] < owners[:, None]).astype(jnp.int32), axis=1)
    return owners * per_pair + jnp.arange(owners.shape[0], dtype=jnp.int32) - owner_start


def pack_kernel(per_pair, me_ref, slots_ref, *refs):
    *value_refs, out_ref = refs
    slots = slots_ref[...]
    me = me_ref[0]
    count, width = slots.shape
    capacity = value_refs[0].shape[0]
    first_row = me * capacity
    lead = slots[:1, :]
    before = jnp.sum((lead < first_row).astype(jnp.float32)).astype(jnp.int32)
    mine = jnp.sum(((lead >= first_row) & (lead < first_row + capacity)).astype(jnp.float32)).astype(jnp.int32)
    moved = pltpu.roll(slots, (width - before) % width, axis=1)
    lane = lax.broadcasted_iota(jnp.int32, slots.shape, 1)
    picked = jnp.where(lane < mine, moved - first_row + 1, 0)
    picked = jnp.concatenate([picked, jnp.zeros((count, capacity - width), jnp.int32)], axis=1)
    reach = per_pair
    while reach < capacity:
        picked = picked + pltpu.roll(picked, reach, axis=1)
        reach *= 2
    row = lax.broadcasted_iota(jnp.int32, picked.shape, 0)
    lane = lax.broadcasted_iota(jnp.int32, picked.shape, 1)
    own = (lane >= row * per_pair) & (lane < (row + 1) * per_pair)
    rows = jnp.sum(jnp.where(own, picked, 0).astype(jnp.float32), axis=0, keepdims=True).astype(jnp.int32) - 1
    chosen = lax.broadcasted_iota(jnp.int32, (capacity, capacity), 0) == rows
    chosen = jnp.where(chosen, 1.0, 0.0).astype(out_ref.dtype)
    first = 0
    for ref in value_refs:
        taken = lax.dot_general(chosen, ref[...], (((0,), (0,)), ((), ())), preferred_element_type=jnp.float32)
        out_ref[:, first : first + ref.shape[1]] = taken.astype(out_ref.dtype)
        first += ref.shape[1]


def pack_rows(source, my_index, dp_count, per_pair, values):
    capacity = values[0].shape[0]
    width = sum(v.shape[1] for v in values)
    slots = source.reshape(dp_count, -1)
    whole = lambda shape: pl.BlockSpec(shape, lambda g, me_ref: (0, 0))
    return pl.pallas_call(
        functools.partial(pack_kernel, per_pair),
        grid_spec=pltpu.PrefetchScalarGridSpec(
            num_scalar_prefetch=1,
            grid=(1,),
            in_specs=[whole(v.shape) for v in (slots, *values)],
            out_specs=whole((capacity, width)),
        ),
        out_shape=jax.ShapeDtypeStruct((capacity, width), values[0].dtype),
        compiler_params=pltpu.CompilerParams(vmem_limit_bytes=60 * 2**20),
    )(my_index.reshape(1), slots, *values)


def take_rows(values, rows):
    chosen = (rows[:, None] == jnp.arange(values.shape[0], dtype=jnp.int32)[None, :]).astype(values.dtype)
    return jnp.dot(chosen, values, preferred_element_type=jnp.float32).astype(values.dtype)


def take_rows_across(values, rows):
    chosen = (rows[:, None] == jnp.arange(values.shape[0], dtype=jnp.int32)[None, :]).astype(values.dtype)
    contract = (((0,), (1,)), ((), ()))
    return lax.dot_general(values, chosen, contract, preferred_element_type=jnp.float32).astype(values.dtype)


def column_of(row_values, tokens):
    return jnp.transpose(jnp.broadcast_to(row_values, (128, tokens)))[:, :1]


def partial_kernel(sizes, arrivals, coded_out, order_ref, rows_ref, query_ref, key_ref, value_ref, *refs):
    contract = (((1,), (1,)), ((), ()))
    query_width = query_ref.shape[1]
    tokens = rows_ref.shape[0]
    step_index = pl.program_id(0)
    part = lax.dot_general(
        rows_ref[:, :query_width], query_ref[...], contract, preferred_element_type=jnp.float32
    )
    others = jnp.concatenate([key_ref[...], value_ref[...]], axis=1)
    part = part + lax.dot_general(
        rows_ref[:, query_width:], others, contract, preferred_element_type=jnp.float32
    )
    for ref in refs[:arrivals]:
        exponent = ref[0, tokens:, :tokens].astype(jnp.int32).astype(jnp.float32)[:1]
        step = jnp.exp2(column_of(exponent, tokens) - FRACTION_BITS)
        part = part + ref[0, :tokens, :].astype(jnp.int32).astype(jnp.float32) * step
    if not coded_out:
        refs[-1][0] = part
        return
    most = jnp.max(jnp.abs(part), axis=1, keepdims=True)
    exponent = jnp.floor(jnp.log2(jnp.maximum(most, 2.0**-100))) + 1.0
    coded = jnp.round(part * jnp.exp2(FRACTION_BITS - exponent))
    coded = jnp.clip(coded, -32767.0, 32767.0).astype(jnp.int32).astype(jnp.int16)
    across = jnp.transpose(jnp.broadcast_to(exponent, (tokens, 128)))[:SCALE_ROWS, :]
    width = coded.shape[1]
    across = jnp.concatenate([across, jnp.zeros((SCALE_ROWS, width - tokens), jnp.float32)], axis=1)
    across = across.astype(jnp.int32).astype(jnp.int16)
    first = 0
    for size, out_ref in zip(sizes, refs[arrivals:]):

        @pl.when((step_index >= first) & (step_index < first + size))
        def _(out_ref=out_ref):
            out_ref[0, :tokens, :] = coded
            out_ref[0, tokens:, :] = across

        first += size


def partials(order, sizes, rows, projections, features, arrived=(), places=None, coded_out=True):
    tokens, width = rows.shape
    steps = sum(sizes)
    coded_block = (1, tokens + SCALE_ROWS, features)
    out_block = coded_block if coded_out else (1, tokens, features)
    kind = jnp.int16 if coded_out else jnp.float32
    plan = [order]
    column = lambda values: plan.append(values.astype(jnp.int32)) or len(plan) - 1
    chosen = lambda g, plan_ref: (plan_ref[g], 0)
    in_turn = lambda first, size: lambda g, plan_ref: (jnp.clip(g - first, 0, size - 1), 0, 0)
    listed = lambda at: lambda g, plan_ref: (plan_ref[at * steps + g], 0, 0)
    arrived_specs = [pl.BlockSpec(coded_block, listed(column(blocks))) for _, blocks in arrived]
    if places is None:
        firsts = [sum(sizes[:i]) for i in range(len(sizes))]
        out_specs = [pl.BlockSpec(out_block, in_turn(f, n)) for f, n in zip(firsts, sizes)]
        out_counts = sizes
    else:
        out_specs = [pl.BlockSpec(out_block, listed(column(places)))]
        out_counts = (places.shape[0] + 1,)
    return pl.pallas_call(
        functools.partial(partial_kernel, sizes, len(arrived), coded_out),
        grid_spec=pltpu.PrefetchScalarGridSpec(
            num_scalar_prefetch=1,
            grid=(steps,),
            in_specs=[pl.BlockSpec((tokens, width), lambda g, plan_ref: (0, 0))]
            + [pl.BlockSpec((features, p.shape[1]), chosen) for p in projections]
            + arrived_specs,
            out_specs=out_specs,
        ),
        out_shape=[jax.ShapeDtypeStruct((n,) + out_block[1:], kind) for n in out_counts],
        compiler_params=pltpu.CompilerParams(vmem_limit_bytes=56 * 2**20),
    )(jnp.concatenate(plan), rows, *projections, *(values for values, _ in arrived))


def sum_kernel(plan_ref, here_ref, *refs):
    out_ref = refs[-1]
    tokens = here_ref.shape[0]
    total = here_ref[...]
    for exponent_ref, coded_ref in zip(refs[:-1:2], refs[1:-1:2]):
        exponent = exponent_ref[0].astype(jnp.int32).astype(jnp.float32)[:1]
        step = jnp.exp2(column_of(exponent, tokens) - FRACTION_BITS)
        total = total + coded_ref[0].astype(jnp.int32).astype(jnp.float32) * step
    out_ref[...] = total


def decoded_sum(here, arrived, places):
    tokens, features = here.shape
    step = features // 2
    columns = pl.BlockSpec((tokens, step), lambda j, plan_ref: (0, j))
    in_specs, operands = [columns], [here]
    for i in range(places.shape[0]):
        in_specs.append(
            pl.BlockSpec((1, SCALE_ROWS, tokens), lambda j, plan_ref, i=i: (plan_ref[i], tokens // SCALE_ROWS, 0))
        )
        in_specs.append(pl.BlockSpec((1, tokens, step), lambda j, plan_ref, i=i: (plan_ref[i], 0, j)))
        operands += [arrived, arrived]
    return pl.pallas_call(
        sum_kernel,
        grid_spec=pltpu.PrefetchScalarGridSpec(
            num_scalar_prefetch=1, grid=(features // step,), in_specs=in_specs, out_specs=columns
        ),
        out_shape=jax.ShapeDtypeStruct((tokens, features), jnp.float32),
        compiler_params=pltpu.CompilerParams(vmem_limit_bytes=60 * 2**20),
    )(places, *operands)


def weight_kernel(plan_ref, pair_ref, right_ref, far_0_ref, far_1_ref, left_ref, back_ref, *out_refs):
    half, tokens = out_refs[0].shape[0], pair_ref.shape[2]
    refs = [(pair_ref, 0), (pair_ref, 1), (right_ref, 0), (right_ref, 1)]
    refs += [(far_0_ref, 0), (far_1_ref, 0), (left_ref, 0), (left_ref, 1)]
    for which, out_ref in zip((1 - plan_ref[0], plan_ref[0]), out_refs):
        mine = pl.ds(pl.multiple_of(which * half, half), half)
        total = 0.0
        for i, (ref, e) in enumerate(refs):
            rows = pl.ds(pl.multiple_of(plan_ref[1 + i] * tokens, tokens), tokens)
            total = total + jnp.dot(ref[e, mine, :], back_ref[rows, :], preferred_element_type=jnp.float32)
        out_ref[...] = total


def weight_halves(core, order, pair, from_right, far, from_left, back_all, step):
    features, tokens = pair.shape[1:]
    width = back_all.shape[1]
    fixed = lambda size: pl.BlockSpec((size, features, tokens), lambda j, plan_ref: (0, 0, 0))
    columns = lambda rows: pl.BlockSpec((rows, step), lambda j, plan_ref: (0, j))
    return pl.pallas_call(
        weight_kernel,
        grid_spec=pltpu.PrefetchScalarGridSpec(
            num_scalar_prefetch=1,
            grid=(width // step,),
            in_specs=[fixed(2), fixed(2), fixed(1), fixed(1), fixed(2), columns(back_all.shape[0])],
            out_specs=[columns(features // 2)] * 2,
        ),
        out_shape=[jax.ShapeDtypeStruct((features // 2, width), jnp.float32)] * 2,
        compiler_params=pltpu.CompilerParams(vmem_limit_bytes=56 * 2**20),
    )(jnp.stack([core, *order]).astype(jnp.int32), pair, from_right, *far, from_left, back_all)


def add_kernel(mine_ref, other_ref, query_ref, key_ref, value_ref):
    total = mine_ref[...] + other_ref[...]
    query_width, key_width = query_ref.shape[1], key_ref.shape[1]
    query_ref[...] = total[:, :query_width]
    key_ref[...] = total[:, query_width : query_width + key_width]
    value_ref[...] = total[:, query_width + key_width :]


def summed_columns(mine, other, widths):
    rows, width = mine.shape
    step = rows // 4
    block = lambda w: pl.BlockSpec((step, w), lambda i: (i, 0))
    return pl.pallas_call(
        add_kernel,
        grid=(rows // step,),
        in_specs=[block(width)] * 2,
        out_specs=[block(w) for w in widths],
        out_shape=[jax.ShapeDtypeStruct((rows, w), mine.dtype) for w in widths],
    )(mine, other)


def shifted(values, axis, by):
    size = lax.axis_size(axis)
    return lax.ppermute(values, axis, [(i, (i + by) % size) for i in range(size)])


def to_feature_owner(values, lows, depth, cores, ring, highs):
    place = lambda y_lo, z, core, x, y_hi: (((y_lo * depth + z) * cores + core) * ring + x) * highs + y_hi
    pairs = []
    for y_lo, z, core, x, y_hi in itertools.product(range(lows), range(depth), range(cores), range(ring), range(highs)):
        owner = x * highs + y_hi
        target = (owner // depth, owner % depth, core, (z + x) % ring, y_lo ^ y_hi ^ (x // 2))
        pairs.append((place(y_lo, z, core, x, y_hi), place(*target)))
    return lax.ppermute(values, DP + TENSOR, pairs)


def body(normed, query_back, key_back, value_back, query_proj, key_proj, value_proj, source):
    y_lo, z, core = (lax.axis_index(a) for a in DP)
    x, y_hi = (lax.axis_index(a) for a in TENSOR)
    lows, depth, cores = (lax.axis_size(a) for a in DP)
    ring, highs = (lax.axis_size(a) for a in TENSOR)
    dp_count, groups = lows * depth * cores, ring * highs
    my_index = (y_lo * depth + z) * cores + core
    capacity, features = normed.shape
    per_pair = capacity // dp_count
    tokens = source.shape[0] // dp_count
    query_width, key_width = query_back.shape[1], key_back.shape[1]
    width = query_width + 2 * key_width
    flat_slots = balanced_slots(source, dp_count, per_pair)

    packed = pack_rows(source, my_index, dp_count, per_pair, (normed, query_back, key_back, value_back))
    packed = packed.reshape(dp_count, per_pair, -1)
    relayed = lax.all_to_all(packed, DP, split_axis=0, concat_axis=0, tiled=True).reshape(capacity, -1)
    back_mine = take_rows(relayed[:, features:], flat_slots)

    inputs_mine = take_rows_across(relayed[:, :features], flat_slots)
    inputs_mine = to_feature_owner(inputs_mine, lows, depth, cores, ring, highs)

    projections = (query_proj, key_proj, value_proj)
    block_at = lambda offsets, y: jnp.stack([(x + s) % ring * highs + y for s in offsets]).astype(jnp.int32)
    away = (2, 1, ring - 1)
    part_of = functools.partial(partials, rows=back_mine, projections=projections, features=features)
    near = part_of(block_at(away + (0,), 1 - y_hi), (len(away), 1))
    other_back = shifted(back_mine, "y_lo", 1)
    inputs_mine, other_back, near = lax.optimization_barrier((inputs_mine, other_back, near))
    copies = jnp.broadcast_to(jnp.stack([back_mine, other_back])[None], (depth, lows) + back_mine.shape)
    inputs_near = shifted(inputs_mine, "y_hi", 1)
    inputs_near, copies, near = lax.optimization_barrier((inputs_near, copies, near))
    pair = jnp.stack([inputs_mine, inputs_near])
    near_away, near_here = [shifted(block, "y_hi", 1) for block in near]
    back_all = lax.all_to_all(copies, "z", split_axis=0, concat_axis=0, tiled=True).reshape(-1, width)
    source_x = y_lo * (depth // highs) + z // highs
    turned = (y_hi + z) % lows
    order = [(x + s - source_x) % depth * lows + (turned + e) % lows for s in range(ring) for e in range(highs)]

    from_left, from_right = shifted(pair, "x", 1), shifted(pair, "x", -1)
    places = jnp.stack([(x + s) % ring for s in away]).astype(jnp.int32)
    (to_others,) = part_of(
        block_at(away, y_hi), (len(away),), arrived=((near_away, jnp.arange(len(away))),), places=places
    )
    far = [shifted(from_left[:1], "x", 1), shifted(from_right[1:], "x", -1)]
    from_others = lax.all_to_all(to_others, "x", split_axis=0, concat_axis=0, tiled=True)
    far, near_here, _ = lax.optimization_barrier((far, near_here, to_others))

    for_other, weight_grad = weight_halves(core, order, pair, from_right, far, from_left, back_all, 2 * key_width)
    from_other = shifted(for_other, "core", 1)
    grads = summed_columns(weight_grad, from_other, (query_width, key_width, key_width))
    (here,) = part_of(block_at((0,), y_hi), (1,), arrived=((near_here, jnp.zeros(1)),), coded_out=False)
    return *grads, decoded_sum(here[0], from_others, places)


def solution(mesh):
    shape = [size for _, size in DP_SIZES + TENSOR_SIZES]
    by_chip = Mesh(mesh.devices.reshape(shape), DP + TENSOR)
    in_specs = (
        P(DP, TENSOR),
        P(DP, TENSOR),
        P(DP, TENSOR),
        P(DP, TENSOR),
        P(None, TENSOR),
        P(None, TENSOR),
        P(None, TENSOR),
        P(),
    )
    out_specs = (P(DP, TENSOR), P(DP, TENSOR), P(DP, TENSOR), P(DP, TENSOR))
    return jax.shard_map(body, mesh=by_chip, in_specs=in_specs, out_specs=out_specs, check_vma=False)
```

```python
import functools
import itertools

import jax
import jax.numpy as jnp
from jax import lax
from jax.experimental import pallas as pl
from jax.experimental.pallas import tpu as pltpu
from jax.sharding import Mesh, PartitionSpec as P

DP_SIZES = (("y_lo", 2), ("z", 4), ("core", 2))
TENSOR_SIZES = (("x", 4), ("y_hi", 2))
DP = tuple(name for name, _ in DP_SIZES)
TENSOR = tuple(name for name, _ in TENSOR_SIZES)
SCALE_ROWS = 16
FRACTION_BITS = 15


def balanced_slots(source, dp_count, per_pair):
    owners = source[: source.shape[0] // dp_count] // (dp_count * per_pair)
    owner_start = jnp.sum((owners[None, :] < owners[:, None]).astype(jnp.int32), axis=1)
    return owners * per_pair + jnp.arange(owners.shape[0], dtype=jnp.int32) - owner_start


def pack_kernel(per_pair, me_ref, slots_ref, *refs):
    *value_refs, out_ref = refs
    slots = slots_ref[...]
    me = me_ref[0]
    count, width = slots.shape
    capacity = value_refs[0].shape[0]
    first_row = me * capacity
    lead = slots[:1, :]
    before = jnp.sum((lead < first_row).astype(jnp.float32)).astype(jnp.int32)
    mine = jnp.sum(((lead >= first_row) & (lead < first_row + capacity)).astype(jnp.float32)).astype(jnp.int32)
    moved = pltpu.roll(slots, (width - before) % width, axis=1)
    lane = lax.broadcasted_iota(jnp.int32, slots.shape, 1)
    picked = jnp.where(lane < mine, moved - first_row + 1, 0)
    picked = jnp.concatenate([picked, jnp.zeros((count, capacity - width), jnp.int32)], axis=1)
    reach = per_pair
    while reach < capacity:
        picked = picked + pltpu.roll(picked, reach, axis=1)
        reach *= 2
    row = lax.broadcasted_iota(jnp.int32, picked.shape, 0)
    lane = lax.broadcasted_iota(jnp.int32, picked.shape, 1)
    own = (lane >= row * per_pair) & (lane < (row + 1) * per_pair)
    rows = jnp.sum(jnp.where(own, picked, 0).astype(jnp.float32), axis=0, keepdims=True).astype(jnp.int32) - 1
    chosen = lax.broadcasted_iota(jnp.int32, (capacity, capacity), 0) == rows
    chosen = jnp.where(chosen, 1.0, 0.0).astype(out_ref.dtype)
    first = 0
    for ref in value_refs:
        taken = lax.dot_general(chosen, ref[...], (((0,), (0,)), ((), ())), preferred_element_type=jnp.float32)
        out_ref[:, first : first + ref.shape[1]] = taken.astype(out_ref.dtype)
        first += ref.shape[1]


def pack_rows(source, my_index, dp_count, per_pair, values):
    capacity = values[0].shape[0]
    width = sum(v.shape[1] for v in values)
    slots = source.reshape(dp_count, -1)
    whole = lambda shape: pl.BlockSpec(shape, lambda g, me_ref: (0, 0))
    return pl.pallas_call(
        functools.partial(pack_kernel, per_pair),
        grid_spec=pltpu.PrefetchScalarGridSpec(
            num_scalar_prefetch=1,
            grid=(1,),
            in_specs=[whole(v.shape) for v in (slots, *values)],
            out_specs=whole((capacity, width)),
        ),
        out_shape=jax.ShapeDtypeStruct((capacity, width), values[0].dtype),
        compiler_params=pltpu.CompilerParams(vmem_limit_bytes=62 * 2**20),
    )(my_index.reshape(1), slots, *values)


def take_rows(values, rows):
    chosen = (rows[:, None] == jnp.arange(values.shape[0], dtype=jnp.int32)[None, :]).astype(values.dtype)
    return jnp.dot(chosen, values, preferred_element_type=jnp.float32).astype(values.dtype)


def take_rows_across(values, rows):
    chosen = (rows[:, None] == jnp.arange(values.shape[0], dtype=jnp.int32)[None, :]).astype(values.dtype)
    contract = (((0,), (1,)), ((), ()))
    return lax.dot_general(values, chosen, contract, preferred_element_type=jnp.float32).astype(values.dtype)


def column_of(row_values, tokens):
    return jnp.transpose(jnp.broadcast_to(row_values, (128, tokens)))[:, :1]


def decoded(coded, exponent, tokens):
    step = jnp.exp2(column_of(exponent.astype(jnp.int32).astype(jnp.float32)[:1], tokens) - FRACTION_BITS)
    return coded.astype(jnp.int32).astype(jnp.float32) * step


def encoded(part):
    tokens, width = part.shape
    most = jnp.max(jnp.abs(part), axis=1, keepdims=True)
    exponent = jnp.floor(jnp.log2(jnp.maximum(most, 2.0**-100))) + 1.0
    coded = jnp.round(part * jnp.exp2(FRACTION_BITS - exponent))
    coded = jnp.clip(coded, -32767.0, 32767.0).astype(jnp.int32).astype(jnp.int16)
    across = jnp.transpose(jnp.broadcast_to(exponent, (tokens, 128)))[:SCALE_ROWS, :]
    across = jnp.concatenate([across, jnp.zeros((SCALE_ROWS, width - tokens), jnp.float32)], axis=1)
    return coded, across.astype(jnp.int32).astype(jnp.int16)


def partial_kernel(sizes, arrivals, coded_out, order_ref, rows_ref, query_ref, key_ref, value_ref, *refs):
    contract = (((1,), (1,)), ((), ()))
    query_width = query_ref.shape[1]
    tokens = rows_ref.shape[0]
    step_index = pl.program_id(0)
    part = lax.dot_general(
        rows_ref[:, :query_width], query_ref[...], contract, preferred_element_type=jnp.float32
    )
    others = jnp.concatenate([key_ref[...], value_ref[...]], axis=1)
    part = part + lax.dot_general(
        rows_ref[:, query_width:], others, contract, preferred_element_type=jnp.float32
    )
    for ref in refs[:arrivals]:
        part = part + decoded(ref[0, :tokens, :], ref[0, tokens:, :tokens], tokens)
    if not coded_out:
        refs[-1][0] = part
        return
    coded, across = encoded(part)
    first = 0
    for size, out_ref in zip(sizes, refs[arrivals:]):

        @pl.when((step_index >= first) & (step_index < first + size))
        def _(out_ref=out_ref):
            out_ref[0, :tokens, :] = coded
            out_ref[0, tokens:, :] = across

        first += size


def partials(order, sizes, rows, projections, features, arrived=(), coded_out=True):
    tokens, width = rows.shape
    coded_block = (1, tokens + SCALE_ROWS, features)
    out_block = coded_block if coded_out else (1, tokens, features)
    kind = jnp.int16 if coded_out else jnp.float32
    chosen = lambda g, order_ref: (order_ref[g], 0)
    in_turn = lambda first, size: lambda g, order_ref: (jnp.clip(g - first, 0, size - 1), 0, 0)
    firsts = [sum(sizes[:i]) for i in range(len(sizes))]
    return pl.pallas_call(
        functools.partial(partial_kernel, sizes, len(arrived), coded_out),
        grid_spec=pltpu.PrefetchScalarGridSpec(
            num_scalar_prefetch=1,
            grid=(sum(sizes),),
            in_specs=[pl.BlockSpec((tokens, width), lambda g, order_ref: (0, 0))]
            + [pl.BlockSpec((features, p.shape[1]), chosen) for p in projections]
            + [pl.BlockSpec(coded_block, lambda g, order_ref: (g, 0, 0)) for _ in arrived],
            out_specs=[pl.BlockSpec(out_block, in_turn(f, n)) for f, n in zip(firsts, sizes)],
        ),
        out_shape=[jax.ShapeDtypeStruct((n,) + out_block[1:], kind) for n in sizes],
        compiler_params=pltpu.CompilerParams(vmem_limit_bytes=56 * 2**20),
    )(order, rows, *projections, *arrived)


def recode_kernel(places_ref, own_ref, near_ref, out_ref):
    tokens = own_ref.shape[1]
    part = own_ref[0] + decoded(near_ref[0, :tokens, :], near_ref[0, tokens:, :tokens], tokens)
    out_ref[0, :tokens, :], out_ref[0, tokens:, :] = encoded(part)


def recoded(own, near, places):
    blocks, tokens, features = own.shape
    coded_block = (1, tokens + SCALE_ROWS, features)
    return pl.pallas_call(
        recode_kernel,
        grid_spec=pltpu.PrefetchScalarGridSpec(
            num_scalar_prefetch=1,
            grid=(blocks,),
            in_specs=[
                pl.BlockSpec((1, tokens, features), lambda g, places_ref: (g, 0, 0)),
                pl.BlockSpec(coded_block, lambda g, places_ref: (g, 0, 0)),
            ],
            out_specs=pl.BlockSpec(coded_block, lambda g, places_ref: (places_ref[g], 0, 0)),
        ),
        out_shape=jax.ShapeDtypeStruct((blocks + 1,) + coded_block[1:], jnp.int16),
        compiler_params=pltpu.CompilerParams(vmem_limit_bytes=56 * 2**20),
    )(places, own, near)


def sum_kernel(plan_ref, here_ref, *refs):
    out_ref = refs[-1]
    tokens = here_ref.shape[0]
    total = here_ref[...]
    for exponent_ref, coded_ref in zip(refs[:-1:2], refs[1:-1:2]):
        total = total + decoded(coded_ref[0], exponent_ref[0], tokens)
    out_ref[...] = total


def decoded_sum(here, arrived, places):
    tokens, features = here.shape
    step = features // 2
    columns = pl.BlockSpec((tokens, step), lambda j, plan_ref: (0, j))
    in_specs, operands = [columns], [here]
    for i in range(places.shape[0]):
        in_specs.append(
            pl.BlockSpec((1, SCALE_ROWS, tokens), lambda j, plan_ref, i=i: (plan_ref[i], tokens // SCALE_ROWS, 0))
        )
        in_specs.append(pl.BlockSpec((1, tokens, step), lambda j, plan_ref, i=i: (plan_ref[i], 0, j)))
        operands += [arrived, arrived]
    return pl.pallas_call(
        sum_kernel,
        grid_spec=pltpu.PrefetchScalarGridSpec(
            num_scalar_prefetch=1, grid=(features // step,), in_specs=in_specs, out_specs=columns
        ),
        out_shape=jax.ShapeDtypeStruct((tokens, features), jnp.float32),
        compiler_params=pltpu.CompilerParams(vmem_limit_bytes=62 * 2**20),
    )(places, *operands)


def weight_kernel(plan_ref, pair_ref, right_ref, far_0_ref, far_1_ref, left_ref, back_ref, *out_refs):
    half, tokens = out_refs[0].shape[0], pair_ref.shape[2]
    refs = [(pair_ref, 0), (pair_ref, 1), (right_ref, 0), (right_ref, 1)]
    refs += [(far_0_ref, 0), (far_1_ref, 0), (left_ref, 0), (left_ref, 1)]
    for which, out_ref in zip((1 - plan_ref[0], plan_ref[0]), out_refs):
        mine = pl.ds(pl.multiple_of(which * half, half), half)
        total = 0.0
        for i, (ref, e) in enumerate(refs):
            rows = pl.ds(pl.multiple_of(plan_ref[1 + i] * tokens, tokens), tokens)
            total = total + jnp.dot(ref[e, mine, :], back_ref[rows, :], preferred_element_type=jnp.float32)
        out_ref[...] = total


def weight_halves(core, order, pair, from_right, far, from_left, back_all, step):
    features, tokens = pair.shape[1:]
    width = back_all.shape[1]
    fixed = lambda size: pl.BlockSpec((size, features, tokens), lambda j, plan_ref: (0, 0, 0))
    columns = lambda rows: pl.BlockSpec((rows, step), lambda j, plan_ref: (0, j))
    return pl.pallas_call(
        weight_kernel,
        grid_spec=pltpu.PrefetchScalarGridSpec(
            num_scalar_prefetch=1,
            grid=(width // step,),
            in_specs=[fixed(2), fixed(2), fixed(1), fixed(1), fixed(2), columns(back_all.shape[0])],
            out_specs=[columns(features // 2)] * 2,
        ),
        out_shape=[jax.ShapeDtypeStruct((features // 2, width), jnp.float32)] * 2,
        compiler_params=pltpu.CompilerParams(vmem_limit_bytes=28 * 2**20),
    )(jnp.stack([core, *order]).astype(jnp.int32), pair, from_right, *far, from_left, back_all)


def add_kernel(mine_ref, other_ref, query_ref, key_ref, value_ref):
    total = mine_ref[...] + other_ref[...]
    query_width, key_width = query_ref.shape[1], key_ref.shape[1]
    query_ref[...] = total[:, :query_width]
    key_ref[...] = total[:, query_width : query_width + key_width]
    value_ref[...] = total[:, query_width + key_width :]


def summed_columns(mine, other, widths):
    rows, width = mine.shape
    step = rows // 4
    block = lambda w: pl.BlockSpec((step, w), lambda i: (i, 0))
    return pl.pallas_call(
        add_kernel,
        grid=(rows // step,),
        in_specs=[block(width)] * 2,
        out_specs=[block(w) for w in widths],
        out_shape=[jax.ShapeDtypeStruct((rows, w), mine.dtype) for w in widths],
    )(mine, other)


def shifted(values, axis, by):
    size = lax.axis_size(axis)
    return lax.ppermute(values, axis, [(i, (i + by) % size) for i in range(size)])


def to_feature_owner(values, turned, lows, depth, cores, ring, highs):
    place = lambda y_lo, z, core, x, y_hi: (((y_lo * depth + z) * cores + core) * ring + x) * highs + y_hi
    pairs = []
    for y_lo, z, core, x, y_hi in itertools.product(range(lows), range(depth), range(cores), range(ring), range(highs)):
        owner = x * highs + y_hi
        target = (owner // depth, owner % depth, core, (z + x) % ring, y_lo ^ y_hi ^ (x // 2) ^ turned)
        pairs.append((place(y_lo, z, core, x, y_hi), place(*target)))
    return lax.ppermute(values, DP + TENSOR, pairs)


def body(normed, query_back, key_back, value_back, query_proj, key_proj, value_proj, source):
    y_lo, z, core = (lax.axis_index(a) for a in DP)
    x, y_hi = (lax.axis_index(a) for a in TENSOR)
    lows, depth, cores = (lax.axis_size(a) for a in DP)
    ring, highs = (lax.axis_size(a) for a in TENSOR)
    dp_count, groups = lows * depth * cores, ring * highs
    my_index = (y_lo * depth + z) * cores + core
    capacity, features = normed.shape
    per_pair = capacity // dp_count
    tokens = source.shape[0] // dp_count
    query_width, key_width = query_back.shape[1], key_back.shape[1]
    width = query_width + 2 * key_width
    flat_slots = balanced_slots(source, dp_count, per_pair)

    packed = pack_rows(source, my_index, dp_count, per_pair, (normed, query_back, key_back, value_back))
    packed = packed.reshape(dp_count, per_pair, -1)
    relayed = lax.all_to_all(packed, DP, split_axis=0, concat_axis=0, tiled=True).reshape(capacity, -1)
    back_mine = take_rows(relayed[:, features:], flat_slots)

    inputs_mine = take_rows_across(relayed[:, :features], flat_slots)
    pair = jnp.stack([to_feature_owner(inputs_mine, turned, lows, depth, cores, ring, highs) for turned in range(highs)])

    projections = (query_proj, key_proj, value_proj)
    block_at = lambda offsets, y: jnp.stack([(x + s) % ring * highs + y for s in offsets]).astype(jnp.int32)
    away = (2, 1, ring - 1)
    part_of = functools.partial(partials, rows=back_mine, projections=projections, features=features)
    near = part_of(block_at(away + (0,), 1 - y_hi), (len(away), 1))
    other_back = shifted(back_mine, "y_lo", 1)
    copies = jnp.broadcast_to(jnp.stack([back_mine, other_back])[None], (depth, lows) + back_mine.shape)
    pair, copies, near = lax.optimization_barrier((pair, copies, near))
    near_away, near_here = [shifted(block, "y_hi", 1) for block in near]
    back_all = lax.all_to_all(copies, "z", split_axis=0, concat_axis=0, tiled=True).reshape(-1, width)
    source_x = y_lo * (depth // highs) + z // highs
    turned = (y_hi + z) % lows
    order = [(x + s - source_x) % depth * lows + (turned + e) % lows for s in range(ring) for e in range(highs)]

    from_left, from_right = shifted(pair, "x", 1), shifted(pair, "x", -1)
    places = jnp.stack([(x + s) % ring for s in away]).astype(jnp.int32)
    (own_away,) = part_of(block_at(away, y_hi), (len(away),), coded_out=False)
    to_others = recoded(own_away, near_away, places)
    far = [shifted(from_left[:1], "x", 1), shifted(from_right[1:], "x", -1)]
    from_others = lax.all_to_all(to_others, "x", split_axis=0, concat_axis=0, tiled=True)
    far, near_here, _ = lax.optimization_barrier((far, near_here, to_others))

    for_other, weight_grad = weight_halves(core, order, pair, from_right, far, from_left, back_all, 2 * key_width)
    from_other = shifted(for_other, "core", 1)
    grads = summed_columns(weight_grad, from_other, (query_width, key_width, key_width))
    (here,) = part_of(block_at((0,), y_hi), (1,), arrived=(near_here,), coded_out=False)
    here, *grads = lax.optimization_barrier((here, *grads))
    return *grads, decoded_sum(here[0], from_others, places)


def solution(mesh):
    shape = [size for _, size in DP_SIZES + TENSOR_SIZES]
    by_chip = Mesh(mesh.devices.reshape(shape), DP + TENSOR)
    in_specs = (
        P(DP, TENSOR),
        P(DP, TENSOR),
        P(DP, TENSOR),
        P(DP, TENSOR),
        P(None, TENSOR),
        P(None, TENSOR),
        P(None, TENSOR),
        P(),
    )
    out_specs = (P(DP, TENSOR), P(DP, TENSOR), P(DP, TENSOR), P(DP, TENSOR))
    return jax.shard_map(body, mesh=by_chip, in_specs=in_specs, out_specs=out_specs, check_vma=False)
```

```python
import functools
import itertools

import jax
import jax.numpy as jnp
from jax import lax
from jax.experimental import pallas as pl
from jax.experimental.pallas import tpu as pltpu
from jax.sharding import Mesh, PartitionSpec as P

DP_SIZES = (("y_lo", 2), ("z", 4), ("core", 2))
TENSOR_SIZES = (("x", 4), ("y_hi", 2))
DP = tuple(name for name, _ in DP_SIZES)
TENSOR = tuple(name for name, _ in TENSOR_SIZES)
SCALE_ROWS = 16
LARGEST = 32766.0
TO_WHOLE = 1.5 * 2.0**23


def balanced_slots(source, dp_count, per_pair):
    owners = source[: source.shape[0] // dp_count] // (dp_count * per_pair)
    owner_start = jnp.sum((owners[None, :] < owners[:, None]).astype(jnp.int32), axis=1)
    return owners * per_pair + jnp.arange(owners.shape[0], dtype=jnp.int32) - owner_start


def pack_kernel(per_pair, me_ref, slots_ref, *refs):
    *value_refs, out_ref = refs
    slots = slots_ref[...]
    me = me_ref[0]
    count, width = slots.shape
    capacity = value_refs[0].shape[0]
    first_row = me * capacity
    lead = slots[:1, :]
    before = jnp.sum((lead < first_row).astype(jnp.float32)).astype(jnp.int32)
    mine = jnp.sum(((lead >= first_row) & (lead < first_row + capacity)).astype(jnp.float32)).astype(jnp.int32)
    moved = pltpu.roll(slots, (width - before) % width, axis=1)
    lane = lax.broadcasted_iota(jnp.int32, slots.shape, 1)
    picked = jnp.where(lane < mine, moved - first_row + 1, 0)
    picked = jnp.concatenate([picked, jnp.zeros((count, capacity - width), jnp.int32)], axis=1)
    reach = per_pair
    while reach < capacity:
        picked = picked + pltpu.roll(picked, reach, axis=1)
        reach *= 2
    row = lax.broadcasted_iota(jnp.int32, picked.shape, 0)
    lane = lax.broadcasted_iota(jnp.int32, picked.shape, 1)
    own = (lane >= row * per_pair) & (lane < (row + 1) * per_pair)
    rows = jnp.sum(jnp.where(own, picked, 0).astype(jnp.float32), axis=0, keepdims=True).astype(jnp.int32) - 1
    chosen = lax.broadcasted_iota(jnp.int32, (capacity, capacity), 0) == rows
    chosen = jnp.where(chosen, 1.0, 0.0).astype(out_ref.dtype)
    first = 0
    for ref in value_refs:
        taken = lax.dot_general(chosen, ref[...], (((0,), (0,)), ((), ())), preferred_element_type=jnp.float32)
        out_ref[:, first : first + ref.shape[1]] = taken.astype(out_ref.dtype)
        first += ref.shape[1]


def pack_rows(source, my_index, dp_count, per_pair, values):
    capacity = values[0].shape[0]
    width = sum(v.shape[1] for v in values)
    slots = source.reshape(dp_count, -1)
    whole = lambda shape: pl.BlockSpec(shape, lambda g, me_ref: (0, 0))
    return pl.pallas_call(
        functools.partial(pack_kernel, per_pair),
        grid_spec=pltpu.PrefetchScalarGridSpec(
            num_scalar_prefetch=1,
            grid=(1,),
            in_specs=[whole(v.shape) for v in (slots, *values)],
            out_specs=whole((capacity, width)),
        ),
        out_shape=jax.ShapeDtypeStruct((capacity, width), values[0].dtype),
        compiler_params=pltpu.CompilerParams(vmem_limit_bytes=62 * 2**20),
    )(my_index.reshape(1), slots, *values)


def take_rows(values, rows):
    chosen = (rows[:, None] == jnp.arange(values.shape[0], dtype=jnp.int32)[None, :]).astype(values.dtype)
    return jnp.dot(chosen, values, preferred_element_type=jnp.float32).astype(values.dtype)


def take_rows_across(values, rows):
    chosen = (rows[:, None] == jnp.arange(values.shape[0], dtype=jnp.int32)[None, :]).astype(values.dtype)
    contract = (((0,), (1,)), ((), ()))
    return lax.dot_general(values, chosen, contract, preferred_element_type=jnp.float32).astype(values.dtype)


def column_of(row_values, tokens):
    return jnp.transpose(jnp.broadcast_to(row_values, (128, tokens)))[:, :1]


def decoded(coded, exponent, tokens):
    exponent = exponent.astype(jnp.int32).astype(jnp.float32)[:1]
    step = jnp.exp2(column_of(exponent, tokens)) * (1.0 / LARGEST)
    return coded.astype(jnp.int32).astype(jnp.float32) * step


def encoded(part):
    tokens, width = part.shape
    most = jnp.max(jnp.abs(part), axis=1, keepdims=True)
    exponent = jnp.floor(jnp.log2(jnp.maximum(most, 2.0**-100))) + 1.0
    scaled = part * (jnp.exp2(-exponent) * LARGEST)
    coded = ((scaled + TO_WHOLE) - TO_WHOLE).astype(jnp.int32).astype(jnp.int16)
    across = jnp.transpose(jnp.broadcast_to(exponent, (tokens, 128)))[:SCALE_ROWS, :]
    across = jnp.concatenate([across, jnp.zeros((SCALE_ROWS, width - tokens), jnp.float32)], axis=1)
    return coded, across.astype(jnp.int32).astype(jnp.int16)


def partial_kernel(sizes, arrivals, coded_out, order_ref, rows_ref, query_ref, key_ref, value_ref, *refs):
    contract = (((1,), (1,)), ((), ()))
    query_width = query_ref.shape[1]
    tokens = rows_ref.shape[0]
    step_index = pl.program_id(0)
    part = lax.dot_general(
        rows_ref[:, :query_width], query_ref[...], contract, preferred_element_type=jnp.float32
    )
    others = jnp.concatenate([key_ref[...], value_ref[...]], axis=1)
    part = part + lax.dot_general(
        rows_ref[:, query_width:], others, contract, preferred_element_type=jnp.float32
    )
    for ref in refs[:arrivals]:
        part = part + decoded(ref[0, :tokens, :], ref[0, tokens:, :tokens], tokens)
    if not coded_out:
        refs[-1][0] = part
        return
    coded, across = encoded(part)
    first = 0
    for size, out_ref in zip(sizes, refs[arrivals:]):

        @pl.when((step_index >= first) & (step_index < first + size))
        def _(out_ref=out_ref):
            out_ref[0, :tokens, :] = coded
            out_ref[0, tokens:, :] = across

        first += size


def partials(order, sizes, rows, projections, features, arrived=(), coded_out=True):
    tokens, width = rows.shape
    coded_block = (1, tokens + SCALE_ROWS, features)
    out_block = coded_block if coded_out else (1, tokens, features)
    kind = jnp.int16 if coded_out else jnp.float32
    chosen = lambda g, order_ref: (order_ref[g], 0)
    in_turn = lambda first, size: lambda g, order_ref: (jnp.clip(g - first, 0, size - 1), 0, 0)
    firsts = [sum(sizes[:i]) for i in range(len(sizes))]
    return pl.pallas_call(
        functools.partial(partial_kernel, sizes, len(arrived), coded_out),
        grid_spec=pltpu.PrefetchScalarGridSpec(
            num_scalar_prefetch=1,
            grid=(sum(sizes),),
            in_specs=[pl.BlockSpec((tokens, width), lambda g, order_ref: (0, 0))]
            + [pl.BlockSpec((features, p.shape[1]), chosen) for p in projections]
            + [pl.BlockSpec(coded_block, lambda g, order_ref: (g, 0, 0)) for _ in arrived],
            out_specs=[pl.BlockSpec(out_block, in_turn(f, n)) for f, n in zip(firsts, sizes)],
        ),
        out_shape=[jax.ShapeDtypeStruct((n,) + out_block[1:], kind) for n in sizes],
        compiler_params=pltpu.CompilerParams(vmem_limit_bytes=56 * 2**20),
    )(order, rows, *projections, *arrived)


def recode_kernel(places_ref, own_ref, near_ref, out_ref):
    tokens = own_ref.shape[1]
    part = own_ref[0] + decoded(near_ref[0, :tokens, :], near_ref[0, tokens:, :tokens], tokens)
    out_ref[0, :tokens, :], out_ref[0, tokens:, :] = encoded(part)


def recoded(own, near, places):
    blocks, tokens, features = own.shape
    coded_block = (1, tokens + SCALE_ROWS, features)
    return pl.pallas_call(
        recode_kernel,
        grid_spec=pltpu.PrefetchScalarGridSpec(
            num_scalar_prefetch=1,
            grid=(blocks,),
            in_specs=[
                pl.BlockSpec((1, tokens, features), lambda g, places_ref: (g, 0, 0)),
                pl.BlockSpec(coded_block, lambda g, places_ref: (g, 0, 0)),
            ],
            out_specs=pl.BlockSpec(coded_block, lambda g, places_ref: (places_ref[g], 0, 0)),
        ),
        out_shape=jax.ShapeDtypeStruct((blocks + 1,) + coded_block[1:], jnp.int16),
        compiler_params=pltpu.CompilerParams(vmem_limit_bytes=56 * 2**20),
    )(places, own, near)


def sum_kernel(plan_ref, here_ref, *refs):
    out_ref = refs[-1]
    tokens = here_ref.shape[0]
    total = here_ref[...]
    for exponent_ref, coded_ref in zip(refs[:-1:2], refs[1:-1:2]):
        total = total + decoded(coded_ref[0], exponent_ref[0], tokens)
    out_ref[...] = total


def decoded_sum(here, arrived, places):
    tokens, features = here.shape
    step = features
    columns = pl.BlockSpec((tokens, step), lambda j, plan_ref: (0, j))
    in_specs, operands = [columns], [here]
    for i in range(places.shape[0]):
        in_specs.append(
            pl.BlockSpec((1, SCALE_ROWS, tokens), lambda j, plan_ref, i=i: (plan_ref[i], tokens // SCALE_ROWS, 0))
        )
        in_specs.append(pl.BlockSpec((1, tokens, step), lambda j, plan_ref, i=i: (plan_ref[i], 0, j)))
        operands += [arrived, arrived]
    return pl.pallas_call(
        sum_kernel,
        grid_spec=pltpu.PrefetchScalarGridSpec(
            num_scalar_prefetch=1, grid=(features // step,), in_specs=in_specs, out_specs=columns
        ),
        out_shape=jax.ShapeDtypeStruct((tokens, features), jnp.float32),
        compiler_params=pltpu.CompilerParams(vmem_limit_bytes=62 * 2**20),
    )(places, *operands)


def weight_kernel(plan_ref, pair_ref, right_ref, far_0_ref, far_1_ref, left_ref, back_ref, *out_refs):
    half, tokens = out_refs[0].shape[0], pair_ref.shape[2]
    refs = [(pair_ref, 0), (pair_ref, 1), (right_ref, 0), (right_ref, 1)]
    refs += [(far_0_ref, 0), (far_1_ref, 0), (left_ref, 0), (left_ref, 1)]
    for which, out_ref in zip((1 - plan_ref[0], plan_ref[0]), out_refs):
        mine = pl.ds(pl.multiple_of(which * half, half), half)
        total = 0.0
        for i, (ref, e) in enumerate(refs):
            rows = pl.ds(pl.multiple_of(plan_ref[1 + i] * tokens, tokens), tokens)
            total = total + jnp.dot(ref[e, mine, :], back_ref[rows, :], preferred_element_type=jnp.float32)
        out_ref[...] = total


def weight_halves(core, order, pair, from_right, far, from_left, back_all, step):
    features, tokens = pair.shape[1:]
    width = back_all.shape[1]
    fixed = lambda size: pl.BlockSpec((size, features, tokens), lambda j, plan_ref: (0, 0, 0))
    columns = lambda rows: pl.BlockSpec((rows, step), lambda j, plan_ref: (0, j))
    return pl.pallas_call(
        weight_kernel,
        grid_spec=pltpu.PrefetchScalarGridSpec(
            num_scalar_prefetch=1,
            grid=(width // step,),
            in_specs=[fixed(2), fixed(2), fixed(1), fixed(1), fixed(2), columns(back_all.shape[0])],
            out_specs=[columns(features // 2)] * 2,
        ),
        out_shape=[jax.ShapeDtypeStruct((features // 2, width), jnp.float32)] * 2,
        compiler_params=pltpu.CompilerParams(vmem_limit_bytes=28 * 2**20),
    )(jnp.stack([core, *order]).astype(jnp.int32), pair, from_right, *far, from_left, back_all)


def add_kernel(mine_ref, other_ref, query_ref, key_ref, value_ref):
    total = mine_ref[...] + other_ref[...]
    query_width, key_width = query_ref.shape[1], key_ref.shape[1]
    query_ref[...] = total[:, :query_width]
    key_ref[...] = total[:, query_width : query_width + key_width]
    value_ref[...] = total[:, query_width + key_width :]


def summed_columns(mine, other, widths):
    rows, width = mine.shape
    step = rows // 4
    block = lambda w: pl.BlockSpec((step, w), lambda i: (i, 0))
    return pl.pallas_call(
        add_kernel,
        grid=(rows // step,),
        in_specs=[block(width)] * 2,
        out_specs=[block(w) for w in widths],
        out_shape=[jax.ShapeDtypeStruct((rows, w), mine.dtype) for w in widths],
    )(mine, other)


def shifted(values, axis, by):
    size = lax.axis_size(axis)
    return lax.ppermute(values, axis, [(i, (i + by) % size) for i in range(size)])


def to_feature_owner(values, turned, lows, depth, cores, ring, highs):
    place = lambda y_lo, z, core, x, y_hi: (((y_lo * depth + z) * cores + core) * ring + x) * highs + y_hi
    pairs = []
    for y_lo, z, core, x, y_hi in itertools.product(range(lows), range(depth), range(cores), range(ring), range(highs)):
        owner = x * highs + y_hi
        target = (owner // depth, owner % depth, core, (z + x) % ring, y_lo ^ y_hi ^ (x // 2) ^ turned)
        pairs.append((place(y_lo, z, core, x, y_hi), place(*target)))
    return lax.ppermute(values, DP + TENSOR, pairs)


def body(normed, query_back, key_back, value_back, query_proj, key_proj, value_proj, source):
    y_lo, z, core = (lax.axis_index(a) for a in DP)
    x, y_hi = (lax.axis_index(a) for a in TENSOR)
    lows, depth, cores = (lax.axis_size(a) for a in DP)
    ring, highs = (lax.axis_size(a) for a in TENSOR)
    dp_count, groups = lows * depth * cores, ring * highs
    my_index = (y_lo * depth + z) * cores + core
    capacity, features = normed.shape
    per_pair = capacity // dp_count
    tokens = source.shape[0] // dp_count
    query_width, key_width = query_back.shape[1], key_back.shape[1]
    width = query_width + 2 * key_width
    flat_slots = balanced_slots(source, dp_count, per_pair)

    packed = pack_rows(source, my_index, dp_count, per_pair, (normed, query_back, key_back, value_back))
    packed = packed.reshape(dp_count, per_pair, -1)
    relayed = lax.all_to_all(packed, DP, split_axis=0, concat_axis=0, tiled=True).reshape(capacity, -1)
    back_mine = take_rows(relayed[:, features:], flat_slots)

    inputs_mine = take_rows_across(relayed[:, :features], flat_slots)
    pair = jnp.stack([to_feature_owner(inputs_mine, turned, lows, depth, cores, ring, highs) for turned in range(highs)])

    projections = (query_proj, key_proj, value_proj)
    block_at = lambda offsets, y: jnp.stack([(x + s) % ring * highs + y for s in offsets]).astype(jnp.int32)
    away = (2, 1, ring - 1)
    part_of = functools.partial(partials, rows=back_mine, projections=projections, features=features)
    other_back = shifted(back_mine, "y_lo", 1)
    copies = jnp.broadcast_to(jnp.stack([back_mine, other_back])[None], (depth, lows) + back_mine.shape)
    rows_after, copies = lax.optimization_barrier((back_mine, copies))
    near = part_of(block_at(away + (0,), 1 - y_hi), (len(away), 1), rows=rows_after)
    pair, copies, near = lax.optimization_barrier((pair, copies, near))
    near_away, near_here = [shifted(block, "y_hi", 1) for block in near]
    back_all = lax.all_to_all(copies, "z", split_axis=0, concat_axis=0, tiled=True).reshape(-1, width)
    source_x = y_lo * (depth // highs) + z // highs
    turned = (y_hi + z) % lows
    order = [(x + s - source_x) % depth * lows + (turned + e) % lows for s in range(ring) for e in range(highs)]

    from_left, from_right = shifted(pair, "x", 1), shifted(pair, "x", -1)
    places = jnp.stack([(x + s) % ring for s in away]).astype(jnp.int32)
    (own_away,) = part_of(block_at(away, y_hi), (len(away),), coded_out=False)
    from_left, from_right, own_away = lax.optimization_barrier((from_left, from_right, own_away))
    to_others = recoded(own_away, near_away, places)
    far = [shifted(from_left[:1], "x", 1), shifted(from_right[1:], "x", -1)]
    from_others = lax.all_to_all(to_others, "x", split_axis=0, concat_axis=0, tiled=True)
    far, near_here, _ = lax.optimization_barrier((far, near_here, to_others))

    for_other, weight_grad = weight_halves(core, order, pair, from_right, far, from_left, back_all, 2 * key_width)
    from_other = shifted(for_other, "core", 1)
    grads = summed_columns(weight_grad, from_other, (query_width, key_width, key_width))
    (here,) = part_of(block_at((0,), y_hi), (1,), arrived=(near_here,), coded_out=False)
    here, *grads = lax.optimization_barrier((here, *grads))
    return *grads, decoded_sum(here[0], from_others, places)


def solution(mesh):
    shape = [size for _, size in DP_SIZES + TENSOR_SIZES]
    by_chip = Mesh(mesh.devices.reshape(shape), DP + TENSOR)
    in_specs = (
        P(DP, TENSOR),
        P(DP, TENSOR),
        P(DP, TENSOR),
        P(DP, TENSOR),
        P(None, TENSOR),
        P(None, TENSOR),
        P(None, TENSOR),
        P(),
    )
    out_specs = (P(DP, TENSOR), P(DP, TENSOR), P(DP, TENSOR), P(DP, TENSOR))
    return jax.shard_map(body, mesh=by_chip, in_specs=in_specs, out_specs=out_specs, check_vma=False)
```

```python
import functools
import itertools

import jax
import jax.numpy as jnp
from jax import lax
from jax.experimental import pallas as pl
from jax.experimental.pallas import tpu as pltpu
from jax.sharding import Mesh, PartitionSpec as P

DP_SIZES = (("y_lo", 2), ("z", 4), ("core", 2))
TENSOR_SIZES = (("x", 4), ("y_hi", 2))
DP = tuple(name for name, _ in DP_SIZES)
TENSOR = tuple(name for name, _ in TENSOR_SIZES)
SCALE_ROWS = 16
LARGEST = 32766.0
TO_WHOLE = 1.5 * 2.0**23


def balanced_slots(source, dp_count, per_pair):
    owners = source[: source.shape[0] // dp_count] // (dp_count * per_pair)
    owner_start = jnp.sum((owners[None, :] < owners[:, None]).astype(jnp.int32), axis=1)
    return owners * per_pair + jnp.arange(owners.shape[0], dtype=jnp.int32) - owner_start


def pack_kernel(per_pair, input_steps, me_ref, slots_ref, inputs_ref, query_ref, key_ref, value_ref, out_ref, chosen_ref):
    capacity = inputs_ref.shape[0]
    count = capacity // per_pair
    here, last = pl.program_id(0), pl.num_programs(0) - 1

    @pl.when(here == 0)
    def _():
        parts = slots_ref.shape[0] // count
        slots = jnp.concatenate([slots_ref[pl.ds(i, count, parts), :] for i in range(parts)], axis=1)
        width = slots.shape[1]
        first_row = me_ref[0] * capacity
        lead = slots[:1, :]
        before = jnp.sum((lead < first_row).astype(jnp.float32)).astype(jnp.int32)
        mine = jnp.sum(((lead >= first_row) & (lead < first_row + capacity)).astype(jnp.float32)).astype(jnp.int32)
        moved = pltpu.roll(slots, (width - before) % width, axis=1)
        lane = lax.broadcasted_iota(jnp.int32, slots.shape, 1)
        picked = jnp.where(lane < mine, moved - first_row + 1, 0)
        picked = jnp.concatenate([picked, jnp.zeros((count, capacity - width), jnp.int32)], axis=1)
        reach = per_pair
        while reach < capacity:
            picked = picked + pltpu.roll(picked, reach, axis=1)
            reach *= 2
        row = lax.broadcasted_iota(jnp.int32, picked.shape, 0)
        lane = lax.broadcasted_iota(jnp.int32, picked.shape, 1)
        own = (lane >= row * per_pair) & (lane < (row + 1) * per_pair)
        rows = jnp.sum(jnp.where(own, picked, 0).astype(jnp.float32), axis=0, keepdims=True) - 1.0
        rows = jnp.transpose(jnp.broadcast_to(rows, (128, capacity)))[:, :1].astype(jnp.int32)
        chosen = lax.broadcasted_iota(jnp.int32, (capacity, capacity), 1) == rows
        chosen_ref[...] = jnp.where(chosen, 1.0, 0.0).astype(chosen_ref.dtype)

    def take(values):
        taken = jnp.dot(chosen_ref[...], values, preferred_element_type=jnp.float32)
        out_ref[...] = taken.astype(out_ref.dtype)

    pl.when(here < input_steps)(lambda: take(inputs_ref[...]))
    pl.when((here >= input_steps) & (here < last))(lambda: take(query_ref[...]))
    pl.when(here == last)(lambda: take(jnp.concatenate([key_ref[...], value_ref[...]], axis=1)))


def pack_rows(source, my_index, per_pair, inputs, query, key, value):
    capacity, features = inputs.shape
    step = 2 * key.shape[1]
    input_steps, query_steps = features // step, query.shape[1] // step
    slots = source.reshape(-1, 128)
    whole = lambda shape: pl.BlockSpec(shape, lambda j, me_ref: (0, 0))
    chunk = lambda first, n: pl.BlockSpec((capacity, step), lambda j, me_ref: (0, jnp.clip(j - first, 0, n - 1)))
    steps = input_steps + query_steps + 1
    return pl.pallas_call(
        functools.partial(pack_kernel, per_pair, input_steps),
        grid_spec=pltpu.PrefetchScalarGridSpec(
            num_scalar_prefetch=1,
            grid=(steps,),
            in_specs=[whole(slots.shape), chunk(0, input_steps), chunk(input_steps, query_steps)]
            + [whole(key.shape), whole(value.shape)],
            out_specs=pl.BlockSpec((capacity, step), lambda j, me_ref: (0, j)),
            scratch_shapes=[pltpu.VMEM((capacity, capacity), inputs.dtype)],
        ),
        out_shape=jax.ShapeDtypeStruct((capacity, steps * step), inputs.dtype),
        compiler_params=pltpu.CompilerParams(vmem_limit_bytes=62 * 2**20),
    )(my_index.reshape(1), slots, inputs, query, key, value)


def take_rows(values, rows):
    chosen = (rows[:, None] == jnp.arange(values.shape[0], dtype=jnp.int32)[None, :]).astype(values.dtype)
    return jnp.dot(chosen, values, preferred_element_type=jnp.float32).astype(values.dtype)


def take_rows_across(values, rows):
    chosen = (rows[:, None] == jnp.arange(values.shape[0], dtype=jnp.int32)[None, :]).astype(values.dtype)
    contract = (((0,), (1,)), ((), ()))
    return lax.dot_general(values, chosen, contract, preferred_element_type=jnp.float32).astype(values.dtype)


def column_of(row_values, tokens):
    return jnp.transpose(jnp.broadcast_to(row_values, (128, tokens)))[:, :1]


def decoded(coded, exponent, tokens):
    exponent = exponent.astype(jnp.int32).astype(jnp.float32)[:1]
    step = jnp.exp2(column_of(exponent, tokens)) * (1.0 / LARGEST)
    return coded.astype(jnp.int32).astype(jnp.float32) * step


def encoded(part):
    tokens, width = part.shape
    most = jnp.max(jnp.abs(part), axis=1, keepdims=True)
    exponent = jnp.floor(jnp.log2(jnp.maximum(most, 2.0**-100))) + 1.0
    scaled = part * (jnp.exp2(-exponent) * LARGEST)
    coded = ((scaled + TO_WHOLE) - TO_WHOLE).astype(jnp.int32).astype(jnp.int16)
    across = jnp.transpose(jnp.broadcast_to(exponent, (tokens, 128)))[:SCALE_ROWS, :]
    across = jnp.concatenate([across, jnp.zeros((SCALE_ROWS, width - tokens), jnp.float32)], axis=1)
    return coded, across.astype(jnp.int32).astype(jnp.int16)


def partial_kernel(sizes, arrivals, coded_out, order_ref, rows_ref, query_ref, key_ref, value_ref, *refs):
    contract = (((1,), (1,)), ((), ()))
    query_width = query_ref.shape[1]
    tokens = rows_ref.shape[0]
    step_index = pl.program_id(0)
    part = lax.dot_general(
        rows_ref[:, :query_width], query_ref[...], contract, preferred_element_type=jnp.float32
    )
    others = jnp.concatenate([key_ref[...], value_ref[...]], axis=1)
    part = part + lax.dot_general(
        rows_ref[:, query_width:], others, contract, preferred_element_type=jnp.float32
    )
    for ref in refs[:arrivals]:
        part = part + decoded(ref[0, :tokens, :], ref[0, tokens:, :tokens], tokens)
    if not coded_out:
        refs[-1][0] = part
        return
    coded, across = encoded(part)
    first = 0
    for size, out_ref in zip(sizes, refs[arrivals:]):

        @pl.when((step_index >= first) & (step_index < first + size))
        def _(out_ref=out_ref):
            out_ref[0, :tokens, :] = coded
            out_ref[0, tokens:, :] = across

        first += size


def partials(order, sizes, rows, projections, features, arrived=(), coded_out=True):
    tokens, width = rows.shape
    coded_block = (1, tokens + SCALE_ROWS, features)
    out_block = coded_block if coded_out else (1, tokens, features)
    kind = jnp.int16 if coded_out else jnp.float32
    chosen = lambda g, order_ref: (order_ref[g], 0)
    in_turn = lambda first, size: lambda g, order_ref: (jnp.clip(g - first, 0, size - 1), 0, 0)
    firsts = [sum(sizes[:i]) for i in range(len(sizes))]
    return pl.pallas_call(
        functools.partial(partial_kernel, sizes, len(arrived), coded_out),
        grid_spec=pltpu.PrefetchScalarGridSpec(
            num_scalar_prefetch=1,
            grid=(sum(sizes),),
            in_specs=[pl.BlockSpec((tokens, width), lambda g, order_ref: (0, 0))]
            + [pl.BlockSpec((features, p.shape[1]), chosen) for p in projections]
            + [pl.BlockSpec(coded_block, lambda g, order_ref: (g, 0, 0)) for _ in arrived],
            out_specs=[pl.BlockSpec(out_block, in_turn(f, n)) for f, n in zip(firsts, sizes)],
        ),
        out_shape=[jax.ShapeDtypeStruct((n,) + out_block[1:], kind) for n in sizes],
        compiler_params=pltpu.CompilerParams(vmem_limit_bytes=56 * 2**20),
    )(order, rows, *projections, *arrived)


def recode_kernel(places_ref, own_ref, near_ref, out_ref):
    tokens = own_ref.shape[1]
    part = own_ref[0] + decoded(near_ref[0, :tokens, :], near_ref[0, tokens:, :tokens], tokens)
    out_ref[0, :tokens, :], out_ref[0, tokens:, :] = encoded(part)


def recoded(own, near, places):
    blocks, tokens, features = own.shape
    coded_block = (1, tokens + SCALE_ROWS, features)
    return pl.pallas_call(
        recode_kernel,
        grid_spec=pltpu.PrefetchScalarGridSpec(
            num_scalar_prefetch=1,
            grid=(blocks,),
            in_specs=[
                pl.BlockSpec((1, tokens, features), lambda g, places_ref: (g, 0, 0)),
                pl.BlockSpec(coded_block, lambda g, places_ref: (g, 0, 0)),
            ],
            out_specs=pl.BlockSpec(coded_block, lambda g, places_ref: (places_ref[g], 0, 0)),
        ),
        out_shape=jax.ShapeDtypeStruct((blocks + 1,) + coded_block[1:], jnp.int16),
        compiler_params=pltpu.CompilerParams(vmem_limit_bytes=56 * 2**20),
    )(places, own, near)


def sum_kernel(plan_ref, here_ref, *refs):
    out_ref = refs[-1]
    tokens = here_ref.shape[0]
    total = here_ref[...]
    for exponent_ref, coded_ref in zip(refs[:-1:2], refs[1:-1:2]):
        total = total + decoded(coded_ref[0], exponent_ref[0], tokens)
    out_ref[...] = total


def decoded_sum(here, arrived, places):
    tokens, features = here.shape
    step = features
    columns = pl.BlockSpec((tokens, step), lambda j, plan_ref: (0, j))
    in_specs, operands = [columns], [here]
    for i in range(places.shape[0]):
        in_specs.append(
            pl.BlockSpec((1, SCALE_ROWS, tokens), lambda j, plan_ref, i=i: (plan_ref[i], tokens // SCALE_ROWS, 0))
        )
        in_specs.append(pl.BlockSpec((1, tokens, step), lambda j, plan_ref, i=i: (plan_ref[i], 0, j)))
        operands += [arrived, arrived]
    return pl.pallas_call(
        sum_kernel,
        grid_spec=pltpu.PrefetchScalarGridSpec(
            num_scalar_prefetch=1, grid=(features // step,), in_specs=in_specs, out_specs=columns
        ),
        out_shape=jax.ShapeDtypeStruct((tokens, features), jnp.float32),
        compiler_params=pltpu.CompilerParams(vmem_limit_bytes=62 * 2**20),
    )(places, *operands)


def weight_kernel(plan_ref, pair_ref, right_ref, far_0_ref, far_1_ref, left_ref, back_ref, *out_refs):
    half, tokens = out_refs[0].shape[0], pair_ref.shape[2]
    refs = [(pair_ref, 0), (pair_ref, 1), (right_ref, 0), (right_ref, 1)]
    refs += [(far_0_ref, 0), (far_1_ref, 0), (left_ref, 0), (left_ref, 1)]
    for which, out_ref in zip((1 - plan_ref[0], plan_ref[0]), out_refs):
        mine = pl.ds(pl.multiple_of(which * half, half), half)
        total = 0.0
        for i, (ref, e) in enumerate(refs):
            rows = pl.ds(pl.multiple_of(plan_ref[1 + i] * tokens, tokens), tokens)
            total = total + jnp.dot(ref[e, mine, :], back_ref[rows, :], preferred_element_type=jnp.float32)
        out_ref[...] = total


def weight_halves(core, order, pair, from_right, far, from_left, back_all, step):
    features, tokens = pair.shape[1:]
    width = back_all.shape[1]
    fixed = lambda size: pl.BlockSpec((size, features, tokens), lambda j, plan_ref: (0, 0, 0))
    columns = lambda rows: pl.BlockSpec((rows, step), lambda j, plan_ref: (0, j))
    return pl.pallas_call(
        weight_kernel,
        grid_spec=pltpu.PrefetchScalarGridSpec(
            num_scalar_prefetch=1,
            grid=(width // step,),
            in_specs=[fixed(2), fixed(2), fixed(1), fixed(1), fixed(2), columns(back_all.shape[0])],
            out_specs=[columns(features // 2)] * 2,
        ),
        out_shape=[jax.ShapeDtypeStruct((features // 2, width), jnp.float32)] * 2,
        compiler_params=pltpu.CompilerParams(vmem_limit_bytes=28 * 2**20),
    )(jnp.stack([core, *order]).astype(jnp.int32), pair, from_right, *far, from_left, back_all)


def add_kernel(mine_ref, other_ref, query_ref, key_ref, value_ref):
    total = mine_ref[...] + other_ref[...]
    query_width, key_width = query_ref.shape[1], key_ref.shape[1]
    query_ref[...] = total[:, :query_width]
    key_ref[...] = total[:, query_width : query_width + key_width]
    value_ref[...] = total[:, query_width + key_width :]


def summed_columns(mine, other, widths):
    rows, width = mine.shape
    step = rows // 4
    block = lambda w: pl.BlockSpec((step, w), lambda i: (i, 0))
    return pl.pallas_call(
        add_kernel,
        grid=(rows // step,),
        in_specs=[block(width)] * 2,
        out_specs=[block(w) for w in widths],
        out_shape=[jax.ShapeDtypeStruct((rows, w), mine.dtype) for w in widths],
    )(mine, other)


def shifted(values, axis, by):
    size = lax.axis_size(axis)
    return lax.ppermute(values, axis, [(i, (i + by) % size) for i in range(size)])


def to_feature_owner(values, turned, lows, depth, cores, ring, highs):
    place = lambda y_lo, z, core, x, y_hi: (((y_lo * depth + z) * cores + core) * ring + x) * highs + y_hi
    pairs = []
    for y_lo, z, core, x, y_hi in itertools.product(range(lows), range(depth), range(cores), range(ring), range(highs)):
        owner = x * highs + y_hi
        target = (owner // depth, owner % depth, core, (z + x) % ring, y_lo ^ y_hi ^ (x // 2) ^ turned)
        pairs.append((place(y_lo, z, core, x, y_hi), place(*target)))
    return lax.ppermute(values, DP + TENSOR, pairs)


def body(normed, query_back, key_back, value_back, query_proj, key_proj, value_proj, source):
    y_lo, z, core = (lax.axis_index(a) for a in DP)
    x, y_hi = (lax.axis_index(a) for a in TENSOR)
    lows, depth, cores = (lax.axis_size(a) for a in DP)
    ring, highs = (lax.axis_size(a) for a in TENSOR)
    dp_count, groups = lows * depth * cores, ring * highs
    my_index = (y_lo * depth + z) * cores + core
    capacity, features = normed.shape
    per_pair = capacity // dp_count
    tokens = source.shape[0] // dp_count
    query_width, key_width = query_back.shape[1], key_back.shape[1]
    width = query_width + 2 * key_width
    flat_slots = balanced_slots(source, dp_count, per_pair)

    packed = pack_rows(source, my_index, per_pair, normed, query_back, key_back, value_back)
    packed = packed.reshape(dp_count, per_pair, -1)
    relayed = lax.all_to_all(packed, DP, split_axis=0, concat_axis=0, tiled=True).reshape(capacity, -1)
    back_mine = take_rows(relayed[:, features:], flat_slots)

    inputs_mine = take_rows_across(relayed[:, :features], flat_slots)
    pair = jnp.stack([to_feature_owner(inputs_mine, turned, lows, depth, cores, ring, highs) for turned in range(highs)])

    projections = (query_proj, key_proj, value_proj)
    block_at = lambda offsets, y: jnp.stack([(x + s) % ring * highs + y for s in offsets]).astype(jnp.int32)
    away = (2, 1, ring - 1)
    part_of = functools.partial(partials, rows=back_mine, projections=projections, features=features)
    other_back = shifted(back_mine, "y_lo", 1)
    copies = jnp.broadcast_to(jnp.stack([back_mine, other_back])[None], (depth, lows) + back_mine.shape)
    rows_after, copies = lax.optimization_barrier((back_mine, copies))
    near = part_of(block_at(away + (0,), 1 - y_hi), (len(away), 1), rows=rows_after)
    pair, copies, near = lax.optimization_barrier((pair, copies, near))
    near_away, near_here = [shifted(block, "y_hi", 1) for block in near]
    back_all = lax.all_to_all(copies, "z", split_axis=0, concat_axis=0, tiled=True).reshape(-1, width)
    source_x = y_lo * (depth // highs) + z // highs
    turned = (y_hi + z) % lows
    order = [(x + s - source_x) % depth * lows + (turned + e) % lows for s in range(ring) for e in range(highs)]

    from_left, from_right = shifted(pair, "x", 1), shifted(pair, "x", -1)
    places = jnp.stack([(x + s) % ring for s in away]).astype(jnp.int32)
    (own_away,) = part_of(block_at(away, y_hi), (len(away),), coded_out=False)
    from_left, from_right, own_away = lax.optimization_barrier((from_left, from_right, own_away))
    to_others = recoded(own_away, near_away, places)
    far = [shifted(from_left[:1], "x", 1), shifted(from_right[1:], "x", -1)]
    from_others = lax.all_to_all(to_others, "x", split_axis=0, concat_axis=0, tiled=True)
    far, near_here, _ = lax.optimization_barrier((far, near_here, to_others))

    for_other, weight_grad = weight_halves(core, order, pair, from_right, far, from_left, back_all, 2 * key_width)
    from_other = shifted(for_other, "core", 1)
    grads = summed_columns(weight_grad, from_other, (query_width, key_width, key_width))
    (here,) = part_of(block_at((0,), y_hi), (1,), arrived=(near_here,), coded_out=False)
    here, *grads = lax.optimization_barrier((here, *grads))
    return *grads, decoded_sum(here[0], from_others, places)


def solution(mesh):
    shape = [size for _, size in DP_SIZES + TENSOR_SIZES]
    by_chip = Mesh(mesh.devices.reshape(shape), DP + TENSOR)
    in_specs = (
        P(DP, TENSOR),
        P(DP, TENSOR),
        P(DP, TENSOR),
        P(DP, TENSOR),
        P(None, TENSOR),
        P(None, TENSOR),
        P(None, TENSOR),
        P(),
    )
    out_specs = (P(DP, TENSOR), P(DP, TENSOR), P(DP, TENSOR), P(DP, TENSOR))
    return jax.shard_map(body, mesh=by_chip, in_specs=in_specs, out_specs=out_specs, check_vma=False)
```

```python
import functools
import itertools

import jax
import jax.numpy as jnp
from jax import lax
from jax.experimental import pallas as pl
from jax.experimental.pallas import tpu as pltpu
from jax.sharding import Mesh, PartitionSpec as P

DP_SIZES = (("y_lo", 2), ("z", 4), ("core", 2))
TENSOR_SIZES = (("x", 4), ("y_hi", 2))
DP = tuple(name for name, _ in DP_SIZES)
TENSOR = tuple(name for name, _ in TENSOR_SIZES)
SCALE_ROWS = 16
LARGEST = 32766.0
TO_WHOLE = 1.5 * 2.0**23


def balanced_slots(source, dp_count, per_pair):
    owners = source[: source.shape[0] // dp_count] // (dp_count * per_pair)
    owner_start = jnp.sum((owners[None, :] < owners[:, None]).astype(jnp.int32), axis=1)
    return owners * per_pair + jnp.arange(owners.shape[0], dtype=jnp.int32) - owner_start


def pack_kernel(per_pair, me_ref, slots_ref, *refs):
    *value_refs, out_ref = refs
    me = me_ref[0]
    capacity = value_refs[0].shape[0]
    count = capacity // per_pair
    parts = slots_ref.shape[0] // count
    slots = jnp.concatenate([slots_ref[pl.ds(i, count, parts), :] for i in range(parts)], axis=1)
    width = slots.shape[1]
    first_row = me * capacity
    lead = slots[:1, :]
    before = jnp.sum((lead < first_row).astype(jnp.float32)).astype(jnp.int32)
    mine = jnp.sum(((lead >= first_row) & (lead < first_row + capacity)).astype(jnp.float32)).astype(jnp.int32)
    moved = pltpu.roll(slots, (width - before) % width, axis=1)
    lane = lax.broadcasted_iota(jnp.int32, slots.shape, 1)
    picked = jnp.where(lane < mine, moved - first_row + 1, 0)
    picked = jnp.concatenate([picked, jnp.zeros((count, capacity - width), jnp.int32)], axis=1)
    reach = per_pair
    while reach < capacity:
        picked = picked + pltpu.roll(picked, reach, axis=1)
        reach *= 2
    row = lax.broadcasted_iota(jnp.int32, picked.shape, 0)
    lane = lax.broadcasted_iota(jnp.int32, picked.shape, 1)
    own = (lane >= row * per_pair) & (lane < (row + 1) * per_pair)
    rows = jnp.sum(jnp.where(own, picked, 0).astype(jnp.float32), axis=0, keepdims=True).astype(jnp.int32) - 1
    chosen = lax.broadcasted_iota(jnp.int32, (capacity, capacity), 0) == rows
    chosen = jnp.where(chosen, 1.0, 0.0).astype(out_ref.dtype)
    first = 0
    for ref in value_refs:
        taken = lax.dot_general(chosen, ref[...], (((0,), (0,)), ((), ())), preferred_element_type=jnp.float32)
        out_ref[:, first : first + ref.shape[1]] = taken.astype(out_ref.dtype)
        first += ref.shape[1]


def pack_rows(source, my_index, per_pair, values):
    capacity = values[0].shape[0]
    width = sum(v.shape[1] for v in values)
    slots = source.reshape(-1, 128)
    whole = lambda shape: pl.BlockSpec(shape, lambda g, me_ref: (0, 0))
    return pl.pallas_call(
        functools.partial(pack_kernel, per_pair),
        grid_spec=pltpu.PrefetchScalarGridSpec(
            num_scalar_prefetch=1,
            grid=(1,),
            in_specs=[whole(v.shape) for v in (slots, *values)],
            out_specs=whole((capacity, width)),
        ),
        out_shape=jax.ShapeDtypeStruct((capacity, width), values[0].dtype),
        compiler_params=pltpu.CompilerParams(vmem_limit_bytes=62 * 2**20),
    )(my_index.reshape(1), slots, *values)


def take_rows(values, rows):
    chosen = (rows[:, None] == jnp.arange(values.shape[0], dtype=jnp.int32)[None, :]).astype(values.dtype)
    return jnp.dot(chosen, values, preferred_element_type=jnp.float32).astype(values.dtype)


def take_rows_across(values, rows):
    chosen = (rows[:, None] == jnp.arange(values.shape[0], dtype=jnp.int32)[None, :]).astype(values.dtype)
    contract = (((0,), (1,)), ((), ()))
    return lax.dot_general(values, chosen, contract, preferred_element_type=jnp.float32).astype(values.dtype)


def column_of(row_values, tokens):
    return jnp.transpose(jnp.broadcast_to(row_values, (128, tokens)))[:, :1]


def decoded(coded, exponent, tokens):
    exponent = exponent.astype(jnp.int32).astype(jnp.float32)[:1]
    step = jnp.exp2(column_of(exponent, tokens)) * (1.0 / LARGEST)
    return coded.astype(jnp.int32).astype(jnp.float32) * step


def encoded(part):
    tokens, width = part.shape
    most = jnp.max(jnp.abs(part), axis=1, keepdims=True)
    exponent = jnp.floor(jnp.log2(jnp.maximum(most, 2.0**-100))) + 1.0
    scaled = part * (jnp.exp2(-exponent) * LARGEST)
    coded = ((scaled + TO_WHOLE) - TO_WHOLE).astype(jnp.int32).astype(jnp.int16)
    across = jnp.transpose(jnp.broadcast_to(exponent, (tokens, 128)))[:SCALE_ROWS, :]
    across = jnp.concatenate([across, jnp.zeros((SCALE_ROWS, width - tokens), jnp.float32)], axis=1)
    return coded, across.astype(jnp.int32).astype(jnp.int16)


def partial_kernel(sizes, arrivals, coded_out, order_ref, rows_ref, query_ref, key_ref, value_ref, *refs):
    contract = (((1,), (1,)), ((), ()))
    query_width = query_ref.shape[1]
    tokens = rows_ref.shape[0]
    step_index = pl.program_id(0)
    part = lax.dot_general(
        rows_ref[:, :query_width], query_ref[...], contract, preferred_element_type=jnp.float32
    )
    others = jnp.concatenate([key_ref[...], value_ref[...]], axis=1)
    part = part + lax.dot_general(
        rows_ref[:, query_width:], others, contract, preferred_element_type=jnp.float32
    )
    for ref in refs[:arrivals]:
        part = part + decoded(ref[0, :tokens, :], ref[0, tokens:, :tokens], tokens)
    if not coded_out:
        refs[-1][0] = part
        return
    coded, across = encoded(part)
    first = 0
    for size, out_ref in zip(sizes, refs[arrivals:]):

        @pl.when((step_index >= first) & (step_index < first + size))
        def _(out_ref=out_ref):
            out_ref[0, :tokens, :] = coded
            out_ref[0, tokens:, :] = across

        first += size


def partials(order, sizes, rows, projections, features, arrived=(), coded_out=True):
    tokens, width = rows.shape
    coded_block = (1, tokens + SCALE_ROWS, features)
    out_block = coded_block if coded_out else (1, tokens, features)
    kind = jnp.int16 if coded_out else jnp.float32
    chosen = lambda g, order_ref: (order_ref[g], 0)
    in_turn = lambda first, size: lambda g, order_ref: (jnp.clip(g - first, 0, size - 1), 0, 0)
    firsts = [sum(sizes[:i]) for i in range(len(sizes))]
    return pl.pallas_call(
        functools.partial(partial_kernel, sizes, len(arrived), coded_out),
        grid_spec=pltpu.PrefetchScalarGridSpec(
            num_scalar_prefetch=1,
            grid=(sum(sizes),),
            in_specs=[pl.BlockSpec((tokens, width), lambda g, order_ref: (0, 0))]
            + [pl.BlockSpec((features, p.shape[1]), chosen) for p in projections]
            + [pl.BlockSpec(coded_block, lambda g, order_ref: (g, 0, 0)) for _ in arrived],
            out_specs=[pl.BlockSpec(out_block, in_turn(f, n)) for f, n in zip(firsts, sizes)],
        ),
        out_shape=[jax.ShapeDtypeStruct((n,) + out_block[1:], kind) for n in sizes],
        compiler_params=pltpu.CompilerParams(vmem_limit_bytes=56 * 2**20),
    )(order, rows, *projections, *arrived)


def recode_kernel(places_ref, own_ref, near_ref, out_ref):
    tokens = own_ref.shape[1]
    part = own_ref[0] + decoded(near_ref[0, :tokens, :], near_ref[0, tokens:, :tokens], tokens)
    out_ref[0, :tokens, :], out_ref[0, tokens:, :] = encoded(part)


def recoded(own, near, places):
    blocks, tokens, features = own.shape
    coded_block = (1, tokens + SCALE_ROWS, features)
    return pl.pallas_call(
        recode_kernel,
        grid_spec=pltpu.PrefetchScalarGridSpec(
            num_scalar_prefetch=1,
            grid=(blocks,),
            in_specs=[
                pl.BlockSpec((1, tokens, features), lambda g, places_ref: (g, 0, 0)),
                pl.BlockSpec(coded_block, lambda g, places_ref: (g, 0, 0)),
            ],
            out_specs=pl.BlockSpec(coded_block, lambda g, places_ref: (places_ref[g], 0, 0)),
        ),
        out_shape=jax.ShapeDtypeStruct((blocks + 1,) + coded_block[1:], jnp.int16),
        compiler_params=pltpu.CompilerParams(vmem_limit_bytes=56 * 2**20),
    )(places, own, near)


def sum_kernel(plan_ref, here_ref, *refs):
    out_ref = refs[-1]
    tokens = here_ref.shape[0]
    total = here_ref[...]
    for exponent_ref, coded_ref in zip(refs[:-1:2], refs[1:-1:2]):
        total = total + decoded(coded_ref[0], exponent_ref[0], tokens)
    out_ref[...] = total


def decoded_sum(here, arrived, places):
    tokens, features = here.shape
    step = features
    columns = pl.BlockSpec((tokens, step), lambda j, plan_ref: (0, j))
    in_specs, operands = [columns], [here]
    for i in range(places.shape[0]):
        in_specs.append(
            pl.BlockSpec((1, SCALE_ROWS, tokens), lambda j, plan_ref, i=i: (plan_ref[i], tokens // SCALE_ROWS, 0))
        )
        in_specs.append(pl.BlockSpec((1, tokens, step), lambda j, plan_ref, i=i: (plan_ref[i], 0, j)))
        operands += [arrived, arrived]
    return pl.pallas_call(
        sum_kernel,
        grid_spec=pltpu.PrefetchScalarGridSpec(
            num_scalar_prefetch=1, grid=(features // step,), in_specs=in_specs, out_specs=columns
        ),
        out_shape=jax.ShapeDtypeStruct((tokens, features), jnp.float32),
        compiler_params=pltpu.CompilerParams(vmem_limit_bytes=62 * 2**20),
    )(places, *operands)


def weight_kernel(plan_ref, pair_ref, right_ref, far_0_ref, far_1_ref, left_ref, back_ref, *out_refs):
    half, tokens = out_refs[0].shape[0], pair_ref.shape[2]
    refs = [(pair_ref, 0), (pair_ref, 1), (right_ref, 0), (right_ref, 1)]
    refs += [(far_0_ref, 0), (far_1_ref, 0), (left_ref, 0), (left_ref, 1)]
    for which, out_ref in zip((1 - plan_ref[0], plan_ref[0]), out_refs):
        mine = pl.ds(pl.multiple_of(which * half, half), half)
        total = 0.0
        for i, (ref, e) in enumerate(refs):
            rows = pl.ds(pl.multiple_of(plan_ref[1 + i] * tokens, tokens), tokens)
            total = total + jnp.dot(ref[e, mine, :], back_ref[rows, :], preferred_element_type=jnp.float32)
        out_ref[...] = total


def weight_halves(core, order, pair, from_right, far, from_left, back_all, step):
    features, tokens = pair.shape[1:]
    width = back_all.shape[1]
    fixed = lambda size: pl.BlockSpec((size, features, tokens), lambda j, plan_ref: (0, 0, 0))
    columns = lambda rows: pl.BlockSpec((rows, step), lambda j, plan_ref: (0, j))
    return pl.pallas_call(
        weight_kernel,
        grid_spec=pltpu.PrefetchScalarGridSpec(
            num_scalar_prefetch=1,
            grid=(width // step,),
            in_specs=[fixed(2), fixed(2), fixed(1), fixed(1), fixed(2), columns(back_all.shape[0])],
            out_specs=[columns(features // 2)] * 2,
        ),
        out_shape=[jax.ShapeDtypeStruct((features // 2, width), jnp.float32)] * 2,
        compiler_params=pltpu.CompilerParams(vmem_limit_bytes=28 * 2**20),
    )(jnp.stack([core, *order]).astype(jnp.int32), pair, from_right, *far, from_left, back_all)


def add_kernel(mine_ref, other_ref, query_ref, key_ref, value_ref):
    total = mine_ref[...] + other_ref[...]
    query_width, key_width = query_ref.shape[1], key_ref.shape[1]
    query_ref[...] = total[:, :query_width]
    key_ref[...] = total[:, query_width : query_width + key_width]
    value_ref[...] = total[:, query_width + key_width :]


def summed_columns(mine, other, widths):
    rows, width = mine.shape
    step = rows // 4
    block = lambda w: pl.BlockSpec((step, w), lambda i: (i, 0))
    return pl.pallas_call(
        add_kernel,
        grid=(rows // step,),
        in_specs=[block(width)] * 2,
        out_specs=[block(w) for w in widths],
        out_shape=[jax.ShapeDtypeStruct((rows, w), mine.dtype) for w in widths],
    )(mine, other)


def shifted(values, axis, by):
    size = lax.axis_size(axis)
    return lax.ppermute(values, axis, [(i, (i + by) % size) for i in range(size)])


def to_feature_owner(values, turned, lows, depth, cores, ring, highs):
    place = lambda y_lo, z, core, x, y_hi: (((y_lo * depth + z) * cores + core) * ring + x) * highs + y_hi
    pairs = []
    for y_lo, z, core, x, y_hi in itertools.product(range(lows), range(depth), range(cores), range(ring), range(highs)):
        owner = x * highs + y_hi
        target = (owner // depth, owner % depth, core, (z + x) % ring, y_lo ^ y_hi ^ (x // 2) ^ turned)
        pairs.append((place(y_lo, z, core, x, y_hi), place(*target)))
    return lax.ppermute(values, DP + TENSOR, pairs)


def body(normed, query_back, key_back, value_back, query_proj, key_proj, value_proj, source):
    y_lo, z, core = (lax.axis_index(a) for a in DP)
    x, y_hi = (lax.axis_index(a) for a in TENSOR)
    lows, depth, cores = (lax.axis_size(a) for a in DP)
    ring, highs = (lax.axis_size(a) for a in TENSOR)
    dp_count, groups = lows * depth * cores, ring * highs
    my_index = (y_lo * depth + z) * cores + core
    capacity, features = normed.shape
    per_pair = capacity // dp_count
    tokens = source.shape[0] // dp_count
    query_width, key_width = query_back.shape[1], key_back.shape[1]
    width = query_width + 2 * key_width
    flat_slots = balanced_slots(source, dp_count, per_pair)

    packed = pack_rows(source, my_index, per_pair, (normed, query_back, key_back, value_back))
    packed = packed.reshape(dp_count, per_pair, -1)
    relayed = lax.all_to_all(packed, DP, split_axis=0, concat_axis=0, tiled=True).reshape(capacity, -1)
    back_mine = take_rows(relayed[:, features:], flat_slots)

    inputs_mine = take_rows_across(relayed[:, :features], flat_slots)
    pair = jnp.stack([to_feature_owner(inputs_mine, turned, lows, depth, cores, ring, highs) for turned in range(highs)])

    projections = (query_proj, key_proj, value_proj)
    block_at = lambda offsets, y: jnp.stack([(x + s) % ring * highs + y for s in offsets]).astype(jnp.int32)
    away = (2, 1, ring - 1)
    part_of = functools.partial(partials, rows=back_mine, projections=projections, features=features)
    other_back = shifted(back_mine, "y_lo", 1)
    copies = jnp.broadcast_to(jnp.stack([back_mine, other_back])[None], (depth, lows) + back_mine.shape)
    rows_after, copies = lax.optimization_barrier((back_mine, copies))
    near = part_of(block_at(away + (0,), 1 - y_hi), (len(away), 1), rows=rows_after)
    pair, copies, near = lax.optimization_barrier((pair, copies, near))
    near_away, near_here = [shifted(block, "y_hi", 1) for block in near]
    back_all = lax.all_to_all(copies, "z", split_axis=0, concat_axis=0, tiled=True).reshape(-1, width)
    source_x = y_lo * (depth // highs) + z // highs
    turned = (y_hi + z) % lows
    order = [(x + s - source_x) % depth * lows + (turned + e) % lows for s in range(ring) for e in range(highs)]

    from_left, from_right = shifted(pair, "x", 1), shifted(pair, "x", -1)
    places = jnp.stack([(x + s) % ring for s in away]).astype(jnp.int32)
    (own_away,) = part_of(block_at(away, y_hi), (len(away),), coded_out=False)
    from_left, from_right, own_away = lax.optimization_barrier((from_left, from_right, own_away))
    to_others = recoded(own_away, near_away, places)
    far = [shifted(from_left[:1], "x", 1), shifted(from_right[1:], "x", -1)]
    from_others = lax.all_to_all(to_others, "x", split_axis=0, concat_axis=0, tiled=True)
    far, near_here, _ = lax.optimization_barrier((far, near_here, to_others))

    for_other, weight_grad = weight_halves(core, order, pair, from_right, far, from_left, back_all, 2 * key_width)
    from_other = shifted(for_other, "core", 1)
    grads = summed_columns(weight_grad, from_other, (query_width, key_width, key_width))
    (here,) = part_of(block_at((0,), y_hi), (1,), arrived=(near_here,), coded_out=False)
    here, *grads = lax.optimization_barrier((here, *grads))
    return *grads, decoded_sum(here[0], from_others, places)


def solution(mesh):
    shape = [size for _, size in DP_SIZES + TENSOR_SIZES]
    by_chip = Mesh(mesh.devices.reshape(shape), DP + TENSOR)
    in_specs = (
        P(DP, TENSOR),
        P(DP, TENSOR),
        P(DP, TENSOR),
        P(DP, TENSOR),
        P(None, TENSOR),
        P(None, TENSOR),
        P(None, TENSOR),
        P(),
    )
    out_specs = (P(DP, TENSOR), P(DP, TENSOR), P(DP, TENSOR), P(DP, TENSOR))
    return jax.shard_map(body, mesh=by_chip, in_specs=in_specs, out_specs=out_specs, check_vma=False)
```

```python
import functools
import itertools

import jax
import jax.numpy as jnp
from jax import lax
from jax.experimental import pallas as pl
from jax.experimental.pallas import tpu as pltpu
from jax.sharding import Mesh, PartitionSpec as P

DP_SIZES = (("y_lo", 2), ("z", 4), ("core", 2))
TENSOR_SIZES = (("x", 4), ("y_hi", 2))
DP = tuple(name for name, _ in DP_SIZES)
TENSOR = tuple(name for name, _ in TENSOR_SIZES)
SCALE_ROWS = 16
LARGEST = 32766.0
TO_WHOLE = 1.5 * 2.0**23


def balanced_slots(source, dp_count, per_pair):
    owners = source[: source.shape[0] // dp_count] // (dp_count * per_pair)
    owner_start = jnp.sum((owners[None, :] < owners[:, None]).astype(jnp.int32), axis=1)
    return owners * per_pair + jnp.arange(owners.shape[0], dtype=jnp.int32) - owner_start


def pack_kernel(per_pair, me_ref, slots_ref, *refs):
    *value_refs, out_ref = refs
    me = me_ref[0]
    capacity = value_refs[0].shape[0]
    count = capacity // per_pair
    parts = slots_ref.shape[0] // count
    slots = jnp.concatenate([slots_ref[pl.ds(i, count, parts), :] for i in range(parts)], axis=1)
    width = slots.shape[1]
    first_row = me * capacity
    lead = slots[:1, :]
    before = jnp.sum((lead < first_row).astype(jnp.float32)).astype(jnp.int32)
    mine = jnp.sum(((lead >= first_row) & (lead < first_row + capacity)).astype(jnp.float32)).astype(jnp.int32)
    moved = pltpu.roll(slots, (width - before) % width, axis=1)
    lane = lax.broadcasted_iota(jnp.int32, slots.shape, 1)
    picked = jnp.where(lane < mine, moved - first_row + 1, 0)
    picked = jnp.concatenate([picked, jnp.zeros((count, capacity - width), jnp.int32)], axis=1)
    reach = per_pair
    while reach < capacity:
        picked = picked + pltpu.roll(picked, reach, axis=1)
        reach *= 2
    row = lax.broadcasted_iota(jnp.int32, picked.shape, 0)
    lane = lax.broadcasted_iota(jnp.int32, picked.shape, 1)
    own = (lane >= row * per_pair) & (lane < (row + 1) * per_pair)
    rows = jnp.sum(jnp.where(own, picked, 0).astype(jnp.float32), axis=0, keepdims=True).astype(jnp.int32) - 1
    chosen = lax.broadcasted_iota(jnp.int32, (capacity, capacity), 0) == rows
    chosen = jnp.where(chosen, 1.0, 0.0).astype(out_ref.dtype)
    first = 0
    for ref in value_refs:
        taken = lax.dot_general(chosen, ref[...], (((0,), (0,)), ((), ())), preferred_element_type=jnp.float32)
        out_ref[:, first : first + ref.shape[1]] = taken.astype(out_ref.dtype)
        first += ref.shape[1]


def pack_rows(source, my_index, per_pair, values):
    capacity = values[0].shape[0]
    width = sum(v.shape[1] for v in values)
    slots = source.reshape(-1, 128)
    whole = lambda shape: pl.BlockSpec(shape, lambda g, me_ref: (0, 0))
    return pl.pallas_call(
        functools.partial(pack_kernel, per_pair),
        grid_spec=pltpu.PrefetchScalarGridSpec(
            num_scalar_prefetch=1,
            grid=(1,),
            in_specs=[whole(v.shape) for v in (slots, *values)],
            out_specs=whole((capacity, width)),
        ),
        out_shape=jax.ShapeDtypeStruct((capacity, width), values[0].dtype),
        compiler_params=pltpu.CompilerParams(vmem_limit_bytes=62 * 2**20),
    )(my_index.reshape(1), slots, *values)


def take_rows(values, rows):
    chosen = (rows[:, None] == jnp.arange(values.shape[0], dtype=jnp.int32)[None, :]).astype(values.dtype)
    return jnp.dot(chosen, values, preferred_element_type=jnp.float32).astype(values.dtype)


def take_rows_across(values, rows):
    chosen = (rows[:, None] == jnp.arange(values.shape[0], dtype=jnp.int32)[None, :]).astype(values.dtype)
    contract = (((0,), (1,)), ((), ()))
    return lax.dot_general(values, chosen, contract, preferred_element_type=jnp.float32).astype(values.dtype)


def column_of(row_values, tokens):
    return jnp.transpose(jnp.broadcast_to(row_values, (128, tokens)))[:, :1]


def decoded(coded, exponent, tokens):
    exponent = exponent.astype(jnp.int32).astype(jnp.float32)[:1]
    step = jnp.exp2(column_of(exponent, tokens)) * (1.0 / LARGEST)
    return coded.astype(jnp.int32).astype(jnp.float32) * step


def encoded(part):
    tokens, width = part.shape
    most = jnp.max(jnp.abs(part), axis=1, keepdims=True)
    exponent = jnp.floor(jnp.log2(jnp.maximum(most, 2.0**-100))) + 1.0
    scaled = part * (jnp.exp2(-exponent) * LARGEST)
    coded = ((scaled + TO_WHOLE) - TO_WHOLE).astype(jnp.int32).astype(jnp.int16)
    across = jnp.transpose(jnp.broadcast_to(exponent, (tokens, 128)))[:SCALE_ROWS, :]
    across = jnp.concatenate([across, jnp.zeros((SCALE_ROWS, width - tokens), jnp.float32)], axis=1)
    return coded, across.astype(jnp.int32).astype(jnp.int16)


def partial_kernel(sizes, arrivals, coded_out, order_ref, rows_ref, query_ref, key_ref, value_ref, *refs):
    contract = (((1,), (1,)), ((), ()))
    query_width = query_ref.shape[1]
    tokens = rows_ref.shape[0]
    step_index = pl.program_id(0)
    part = lax.dot_general(
        rows_ref[:, :query_width], query_ref[...], contract, preferred_element_type=jnp.float32
    )
    others = jnp.concatenate([key_ref[...], value_ref[...]], axis=1)
    part = part + lax.dot_general(
        rows_ref[:, query_width:], others, contract, preferred_element_type=jnp.float32
    )
    for ref in refs[:arrivals]:
        part = part + decoded(ref[0, :tokens, :], ref[0, tokens:, :tokens], tokens)
    if not coded_out:
        refs[-1][0] = part
        return
    coded, across = encoded(part)
    first = 0
    for size, out_ref in zip(sizes, refs[arrivals:]):

        @pl.when((step_index >= first) & (step_index < first + size))
        def _(out_ref=out_ref):
            out_ref[0, :tokens, :] = coded
            out_ref[0, tokens:, :] = across

        first += size


def partials(order, sizes, rows, projections, features, arrived=(), coded_out=True):
    tokens, width = rows.shape
    coded_block = (1, tokens + SCALE_ROWS, features)
    out_block = coded_block if coded_out else (1, tokens, features)
    kind = jnp.int16 if coded_out else jnp.float32
    chosen = lambda g, order_ref: (order_ref[g], 0)
    in_turn = lambda first, size: lambda g, order_ref: (jnp.clip(g - first, 0, size - 1), 0, 0)
    firsts = [sum(sizes[:i]) for i in range(len(sizes))]
    return pl.pallas_call(
        functools.partial(partial_kernel, sizes, len(arrived), coded_out),
        grid_spec=pltpu.PrefetchScalarGridSpec(
            num_scalar_prefetch=1,
            grid=(sum(sizes),),
            in_specs=[pl.BlockSpec((tokens, width), lambda g, order_ref: (0, 0))]
            + [pl.BlockSpec((features, p.shape[1]), chosen) for p in projections]
            + [pl.BlockSpec(coded_block, lambda g, order_ref: (g, 0, 0)) for _ in arrived],
            out_specs=[pl.BlockSpec(out_block, in_turn(f, n)) for f, n in zip(firsts, sizes)],
        ),
        out_shape=[jax.ShapeDtypeStruct((n,) + out_block[1:], kind) for n in sizes],
        compiler_params=pltpu.CompilerParams(vmem_limit_bytes=56 * 2**20),
    )(order, rows, *projections, *arrived)


def recode_kernel(places_ref, own_ref, near_ref, out_ref):
    tokens = own_ref.shape[1]
    part = own_ref[0] + decoded(near_ref[0, :tokens, :], near_ref[0, tokens:, :tokens], tokens)
    out_ref[0, :tokens, :], out_ref[0, tokens:, :] = encoded(part)


def recoded(own, near, places):
    blocks, tokens, features = own.shape
    coded_block = (1, tokens + SCALE_ROWS, features)
    return pl.pallas_call(
        recode_kernel,
        grid_spec=pltpu.PrefetchScalarGridSpec(
            num_scalar_prefetch=1,
            grid=(blocks,),
            in_specs=[
                pl.BlockSpec((1, tokens, features), lambda g, places_ref: (g, 0, 0)),
                pl.BlockSpec(coded_block, lambda g, places_ref: (g, 0, 0)),
            ],
            out_specs=pl.BlockSpec(coded_block, lambda g, places_ref: (places_ref[g], 0, 0)),
        ),
        out_shape=jax.ShapeDtypeStruct((blocks + 1,) + coded_block[1:], jnp.int16),
        compiler_params=pltpu.CompilerParams(vmem_limit_bytes=28 * 2**20),
    )(places, own, near)


def sum_kernel(plan_ref, here_ref, *refs):
    out_ref = refs[-1]
    tokens = here_ref.shape[0]
    total = here_ref[...]
    for exponent_ref, coded_ref in zip(refs[:-1:2], refs[1:-1:2]):
        total = total + decoded(coded_ref[0], exponent_ref[0], tokens)
    out_ref[...] = total


def decoded_sum(here, arrived, places):
    tokens, features = here.shape
    step = features
    columns = pl.BlockSpec((tokens, step), lambda j, plan_ref: (0, j))
    in_specs, operands = [columns], [here]
    for i in range(places.shape[0]):
        in_specs.append(
            pl.BlockSpec((1, SCALE_ROWS, tokens), lambda j, plan_ref, i=i: (plan_ref[i], tokens // SCALE_ROWS, 0))
        )
        in_specs.append(pl.BlockSpec((1, tokens, step), lambda j, plan_ref, i=i: (plan_ref[i], 0, j)))
        operands += [arrived, arrived]
    return pl.pallas_call(
        sum_kernel,
        grid_spec=pltpu.PrefetchScalarGridSpec(
            num_scalar_prefetch=1, grid=(features // step,), in_specs=in_specs, out_specs=columns
        ),
        out_shape=jax.ShapeDtypeStruct((tokens, features), jnp.float32),
        compiler_params=pltpu.CompilerParams(vmem_limit_bytes=62 * 2**20),
    )(places, *operands)


def weight_kernel(plan_ref, pair_ref, right_ref, far_0_ref, far_1_ref, left_ref, back_ref, *out_refs):
    half, tokens = out_refs[0].shape[0], pair_ref.shape[2]
    refs = [(pair_ref, 0), (pair_ref, 1), (right_ref, 0), (right_ref, 1)]
    refs += [(far_0_ref, 0), (far_1_ref, 0), (left_ref, 0), (left_ref, 1)]
    for which, out_ref in zip((1 - plan_ref[0], plan_ref[0]), out_refs):
        mine = pl.ds(pl.multiple_of(which * half, half), half)
        total = 0.0
        for i, (ref, e) in enumerate(refs):
            rows = pl.ds(pl.multiple_of(plan_ref[1 + i] * tokens, tokens), tokens)
            total = total + jnp.dot(ref[e, mine, :], back_ref[rows, :], preferred_element_type=jnp.float32)
        out_ref[...] = total


def weight_halves(core, order, pair, from_right, far, from_left, back_all, step):
    features, tokens = pair.shape[1:]
    width = back_all.shape[1]
    fixed = lambda size: pl.BlockSpec((size, features, tokens), lambda j, plan_ref: (0, 0, 0))
    columns = lambda rows: pl.BlockSpec((rows, step), lambda j, plan_ref: (0, j))
    return pl.pallas_call(
        weight_kernel,
        grid_spec=pltpu.PrefetchScalarGridSpec(
            num_scalar_prefetch=1,
            grid=(width // step,),
            in_specs=[fixed(2), fixed(2), fixed(1), fixed(1), fixed(2), columns(back_all.shape[0])],
            out_specs=[columns(features // 2)] * 2,
        ),
        out_shape=[jax.ShapeDtypeStruct((features // 2, width), jnp.float32)] * 2,
        compiler_params=pltpu.CompilerParams(vmem_limit_bytes=28 * 2**20),
    )(jnp.stack([core, *order]).astype(jnp.int32), pair, from_right, *far, from_left, back_all)


def add_kernel(mine_ref, other_ref, query_ref, key_ref, value_ref):
    total = mine_ref[...] + other_ref[...]
    query_width, key_width = query_ref.shape[1], key_ref.shape[1]
    query_ref[...] = total[:, :query_width]
    key_ref[...] = total[:, query_width : query_width + key_width]
    value_ref[...] = total[:, query_width + key_width :]


def summed_columns(mine, other, widths):
    rows, width = mine.shape
    step = rows // 4
    block = lambda w: pl.BlockSpec((step, w), lambda i: (i, 0))
    return pl.pallas_call(
        add_kernel,
        grid=(rows // step,),
        in_specs=[block(width)] * 2,
        out_specs=[block(w) for w in widths],
        out_shape=[jax.ShapeDtypeStruct((rows, w), mine.dtype) for w in widths],
    )(mine, other)


def shifted(values, axis, by):
    size = lax.axis_size(axis)
    return lax.ppermute(values, axis, [(i, (i + by) % size) for i in range(size)])


def to_feature_owner(values, turned, lows, depth, cores, ring, highs):
    place = lambda y_lo, z, core, x, y_hi: (((y_lo * depth + z) * cores + core) * ring + x) * highs + y_hi
    pairs = []
    for y_lo, z, core, x, y_hi in itertools.product(range(lows), range(depth), range(cores), range(ring), range(highs)):
        owner = x * highs + y_hi
        target = (owner // depth, owner % depth, core, (z + x) % ring, y_lo ^ y_hi ^ (x // 2) ^ turned)
        pairs.append((place(y_lo, z, core, x, y_hi), place(*target)))
    return lax.ppermute(values, DP + TENSOR, pairs)


def body(normed, query_back, key_back, value_back, query_proj, key_proj, value_proj, source):
    y_lo, z, core = (lax.axis_index(a) for a in DP)
    x, y_hi = (lax.axis_index(a) for a in TENSOR)
    lows, depth, cores = (lax.axis_size(a) for a in DP)
    ring, highs = (lax.axis_size(a) for a in TENSOR)
    dp_count, groups = lows * depth * cores, ring * highs
    my_index = (y_lo * depth + z) * cores + core
    capacity, features = normed.shape
    per_pair = capacity // dp_count
    tokens = source.shape[0] // dp_count
    query_width, key_width = query_back.shape[1], key_back.shape[1]
    width = query_width + 2 * key_width
    flat_slots = balanced_slots(source, dp_count, per_pair)

    packed = pack_rows(source, my_index, per_pair, (normed, query_back, key_back, value_back))
    packed = packed.reshape(dp_count, per_pair, -1)
    relayed = lax.all_to_all(packed, DP, split_axis=0, concat_axis=0, tiled=True).reshape(capacity, -1)
    back_mine = take_rows(relayed[:, features:], flat_slots)

    inputs_mine = take_rows_across(relayed[:, :features], flat_slots)
    pair = jnp.stack([to_feature_owner(inputs_mine, turned, lows, depth, cores, ring, highs) for turned in range(highs)])

    projections = (query_proj, key_proj, value_proj)
    block_at = lambda offsets, y: jnp.stack([(x + s) % ring * highs + y for s in offsets]).astype(jnp.int32)
    away = (2, 1, ring - 1)
    part_of = functools.partial(partials, rows=back_mine, projections=projections, features=features)
    other_back = shifted(back_mine, "y_lo", 1)
    copies = jnp.broadcast_to(jnp.stack([back_mine, other_back])[None], (depth, lows) + back_mine.shape)
    rows_after, copies = lax.optimization_barrier((back_mine, copies))
    near = part_of(block_at(away + (0,), 1 - y_hi), (len(away), 1), rows=rows_after)
    pair, copies, near = lax.optimization_barrier((pair, copies, near))
    near_away, near_here = [shifted(block, "y_hi", 1) for block in near]
    back_all = lax.all_to_all(copies, "z", split_axis=0, concat_axis=0, tiled=True).reshape(-1, width)
    source_x = y_lo * (depth // highs) + z // highs
    turned = (y_hi + z) % lows
    order = [(x + s - source_x) % depth * lows + (turned + e) % lows for s in range(ring) for e in range(highs)]

    from_left, from_right = shifted(pair, "x", 1), shifted(pair, "x", -1)
    places = jnp.stack([(x + s) % ring for s in away]).astype(jnp.int32)
    (own_away,) = part_of(block_at(away, y_hi), (len(away),), coded_out=False)
    from_left, from_right, own_away = lax.optimization_barrier((from_left, from_right, own_away))
    to_others = recoded(own_away, near_away, places)
    far = [shifted(from_left[:1], "x", 1), shifted(from_right[1:], "x", -1)]
    from_others = lax.all_to_all(to_others, "x", split_axis=0, concat_axis=0, tiled=True)
    far, near_here, _ = lax.optimization_barrier((far, near_here, to_others))

    for_other, weight_grad = weight_halves(core, order, pair, from_right, far, from_left, back_all, 2 * key_width)
    from_other = shifted(for_other, "core", 1)
    grads = summed_columns(weight_grad, from_other, (query_width, key_width, key_width))
    (here,) = part_of(block_at((0,), y_hi), (1,), arrived=(near_here,), coded_out=False)
    here, *grads = lax.optimization_barrier((here, *grads))
    return *grads, decoded_sum(here[0], from_others, places)


def solution(mesh):
    shape = [size for _, size in DP_SIZES + TENSOR_SIZES]
    by_chip = Mesh(mesh.devices.reshape(shape), DP + TENSOR)
    in_specs = (
        P(DP, TENSOR),
        P(DP, TENSOR),
        P(DP, TENSOR),
        P(DP, TENSOR),
        P(None, TENSOR),
        P(None, TENSOR),
        P(None, TENSOR),
        P(),
    )
    out_specs = (P(DP, TENSOR), P(DP, TENSOR), P(DP, TENSOR), P(DP, TENSOR))
    return jax.shard_map(body, mesh=by_chip, in_specs=in_specs, out_specs=out_specs, check_vma=False)
```
